128 devices in a mesh: tensor: 4 (over x), dp: 16 (over z, y), outer: 2 (over core).
Axes of the slice: x: 4, y: 4, z: 4, core: 2. Of those that a mesh axis runs over, the one named last changes fastest.
Arguments:
- hidden_act: bfloat16 [8192, 14336], P(('dp', 'outer'), 'tensor'), may hold values from -6 to 6
- out_grad: bfloat16 [8192, 6144], P(('dp', 'outer')), may hold values from -6 to 6
- start_vectors: float32 [16, 6144], replicated, may hold values from -6 to 6
- kept_counts: int32 [4, 2, 16], P('tensor', 'outer', 'dp'), may hold values from 1 to 16, as said below
Outputs:
- synced_grad: bfloat16 [14336, 6144], P('tensor', 'outer')
The draws below stay inside these ranges and needn't reach their ends.
Inputs may be any that keep to these rules, and one draw needn't show every extreme that they name: kept_counts[t, q, e] is how many atoms pod q keeps for piece (t, e); for some t and e every pod keeps 16, and some entry is 1.
All inputs are finite; a program needn't handle non-finite values.
Results may differ from the reference program's by a relative error of at most 0.039.
Values may be sent and summed in bfloat16 or wider, within the bound.
A program may use at most 256 MiB of HBM per device.

```python
import math
import jax
import jax.numpy as jnp
from jax import lax

D = 6144
HID = 14336
TOK_DEV = 256
ATOMS = 16
POWER = 2
POD_TOKENS = 4096
TOKENS = 8192
N_TENSOR = 4
N_DP = 16
N_OUTER = 2


def draw_kept_counts(key, part):
    key = jax.random.fold_in(key, 7)
    subkeys = jax.random.split(key, 4)
    grid_shape = (N_TENSOR, N_OUTER, N_DP)
    counts = jax.random.randint(subkeys[0], grid_shape, 1, ATOMS + 1, dtype=jnp.int32)
    tensor_pick = jax.random.randint(subkeys[1], (), 0, N_TENSOR, dtype=jnp.int32)
    member_pick = jax.random.randint(subkeys[2], (), 0, N_DP, dtype=jnp.int32)
    pod_pick = jax.random.randint(subkeys[3], (), 0, N_OUTER, dtype=jnp.int32)
    tensor_ids = lax.broadcasted_iota(jnp.int32, grid_shape, 0)
    pod_ids = lax.broadcasted_iota(jnp.int32, grid_shape, 1)
    member_ids = lax.broadcasted_iota(jnp.int32, grid_shape, 2)
    full_column = (tensor_ids == tensor_pick) & (member_ids == member_pick)
    counts = jnp.where(full_column, ATOMS, counts)
    lowest = (tensor_ids == (tensor_pick + 1) % N_TENSOR) & (pod_ids == pod_pick) & (member_ids == member_pick)
    counts = jnp.where(lowest, 1, counts)
    return counts.astype(jnp.int32)


def shard_levels(rng, shape, shards, smallest, top_value):
    factor_of, own = 1.0, jax.random.fold_in(rng, 6)
    for position, parts in shards:
        draws = jnp.exp(jax.random.uniform(jax.random.fold_in(own, position), (parts,), jnp.float32, smallest / len(shards), top_value / len(shards)))
        factor_of = factor_of * jnp.repeat(draws, shape[position] // parts).reshape([-1 if axis == position else 1 for axis in range(len(shape))])
    return factor_of


def noise(key, dims, deviation, reach, pieces=(), held_as=jnp.bfloat16):
    drawn = deviation * jax.random.normal(key, dims, jnp.float32)
    if pieces:
        drawn = drawn * shard_levels(key, dims, pieces, -0.22, 0.18)
    return jnp.clip(drawn, -reach, reach).astype(held_as)


def setup_inputs(seed: int = 0) -> dict:
    key_of = jax.random.split(jax.random.key(seed), 5)
    hidden_act = noise(key_of[0], (TOKENS, HID), 1.0, 6.0, ((0, 32), (1, 4)))
    out_grad = noise(key_of[1], (TOKENS, D), 1.0, 6.0, ((0, 32),))
    start_vectors = noise(key_of[2], (ATOMS, D), 1.0, 6.0, (), jnp.float32)
    kept_counts = draw_kept_counts(jax.random.fold_in(key_of[4], 71), 0)
    return dict(hidden_act=hidden_act, out_grad=out_grad, start_vectors=start_vectors, kept_counts=kept_counts)


PRECISE = lax.Precision.HIGHEST

def compress(owned_piece, start_vectors, kept_number):
    atom_count = start_vectors.shape[0]
    right_side = start_vectors
    left_side = None
    for repeat in range(POWER):
        left_side = lax.dot_general(right_side, owned_piece, (((1,), (1,)), ((), ())), precision=PRECISE)
        gram_matrix = jnp.dot(left_side, left_side.T, precision=PRECISE)
        ridge_term = 1e-05 * jnp.trace(gram_matrix) / atom_count
        factor = jnp.linalg.cholesky(gram_matrix + ridge_term * jnp.eye(atom_count, dtype=gram_matrix.dtype))
        left_side = jax.scipy.linalg.solve_triangular(factor, left_side, lower=True)
        right_side = jnp.dot(left_side, owned_piece, precision=PRECISE)
    keep_mask = (jnp.arange(atom_count, dtype=jnp.int32) < kept_number)[:, None]
    left_atoms = jnp.where(keep_mask, left_side, 0.0).astype(jnp.bfloat16)
    right_atoms = jnp.where(keep_mask, right_side, 0.0).astype(jnp.bfloat16)
    return (left_atoms, right_atoms)

def reference(hidden_act, out_grad, start_vectors, kept_counts):
    hidden_rows = HID // N_TENSOR
    own_rows = hidden_rows // N_DP
    activations = hidden_act.reshape(N_DP, N_OUTER, TOK_DEV, N_TENSOR, hidden_rows)
    gradients = out_grad.reshape(N_DP, N_OUTER, TOK_DEV, D)
    grad_scale = 1.0 / math.sqrt(POD_TOKENS)

    def tensor_block(tensor_index):

        def pod_step(running, pod_index):
            pod_grad = jnp.zeros((hidden_rows, D), jnp.float32)
            for member in range(N_DP):
                act_block = activations[member, pod_index, :, tensor_index]
                grad_block = gradients[member, pod_index]
                partial_term = lax.dot_general(act_block.astype(jnp.float32), grad_block.astype(jnp.float32), (((0,), (0,)), ((), ())), preferred_element_type=jnp.float32) * grad_scale
                pod_grad = pod_grad + lax.optimization_barrier(partial_term.astype(jnp.bfloat16)).astype(jnp.float32)
            rebuilt = []
            for owner in range(N_DP):
                owned_piece = pod_grad[owner * own_rows:(owner + 1) * own_rows]
                left_atoms, right_atoms = compress(owned_piece, start_vectors, kept_counts[tensor_index, pod_index, owner])
                rebuilt.append(jnp.dot(left_atoms.T.astype(jnp.float32), right_atoms.astype(jnp.float32), preferred_element_type=jnp.float32))
            return (running + jnp.concatenate(rebuilt, 0), None)
        initial = jnp.zeros((hidden_rows, D), jnp.float32)
        summed, unused = lax.scan(pod_step, initial, jnp.arange(N_OUTER, dtype=jnp.int32))
        return summed.astype(jnp.bfloat16)
    blocks = lax.map(tensor_block, jnp.arange(N_TENSOR, dtype=jnp.int32))
    return blocks.reshape(HID, D)
```

```python
import math

import jax
import jax.numpy as jnp
from jax import lax
from jax.sharding import PartitionSpec as P

TOK_DEV = 256
POWER = 2


PRECISE = lax.Precision.HIGHEST


def orthonormal(left_side):
    atom_count = left_side.shape[0]
    gram_matrix = jnp.dot(left_side, left_side.T, precision=PRECISE)
    ridge_term = 1e-05 * jnp.trace(gram_matrix) / atom_count
    factor = jnp.linalg.cholesky(
        gram_matrix + ridge_term * jnp.eye(atom_count, dtype=gram_matrix.dtype)
    )
    return jax.scipy.linalg.solve_triangular(factor, left_side, lower=True)


def shards(hidden_act, out_grad, start_vectors, kept_counts):
    token_count, feature_count = out_grad.shape
    atom_count = start_vectors.shape[0]
    member_count = lax.axis_size("dp")
    pod_count = lax.axis_size("outer")
    pod_width = feature_count // pod_count
    own_rows = hidden_act.shape[1] // member_count
    grad_scale = 1.0 / math.sqrt(TOK_DEV * member_count)
    hidden = hidden_act.reshape(token_count, member_count, own_rows)
    hidden_wide = hidden.astype(jnp.float32)
    grad_wide = out_grad.astype(jnp.float32)

    token_side = lax.dot_general(
        start_vectors, grad_wide, (((1,), (1,)), ((), ())), precision=PRECISE
    )
    left_side = jnp.einsum("at,ter->ear", token_side, hidden_wide, precision=PRECISE)
    for repeat in range(POWER):
        left_side = lax.psum_scatter(left_side, "dp", scatter_dimension=0, tiled=True)[0] * grad_scale
        left_side = orthonormal(left_side)
        if repeat == POWER - 1:
            keep_mask = jnp.arange(atom_count, dtype=jnp.int32) < kept_counts[0, 0, 0]
            left_side = jnp.where(keep_mask[:, None], left_side, 0.0)
        all_left = lax.all_gather(left_side, "dp", axis=0)
        token_side = jnp.einsum("ear,ter->eat", all_left, hidden_wide, precision=PRECISE) * grad_scale
        token_side = token_side.reshape(member_count * atom_count, token_count)
        right_part = jnp.dot(
            token_side.astype(jnp.bfloat16), out_grad, preferred_element_type=jnp.float32
        ).astype(jnp.bfloat16)
        if repeat < POWER - 1:
            right_side = lax.psum(right_part, "dp")
            token_side = lax.dot_general(
                right_side, out_grad, (((1,), (1,)), ((), ())), preferred_element_type=jnp.float32
            ).reshape(member_count, atom_count, token_count)
            left_side = jnp.einsum("eat,ter->ear", token_side, hidden_wide, precision=PRECISE)
        else:
            right_side = lax.psum_scatter(right_part, "dp", scatter_dimension=0, tiled=True)
    all_left = lax.all_gather(all_left.astype(jnp.bfloat16), "outer", axis=1)
    both_right = lax.all_to_all(right_side, "outer", split_axis=1, concat_axis=0, tiled=True)
    all_right = lax.all_gather(both_right, "dp", axis=0)
    rebuilt = jnp.einsum(
        "ekr,ekc->erc",
        all_left.reshape(member_count, pod_count * atom_count, own_rows),
        all_right.reshape(member_count, pod_count * atom_count, pod_width),
        preferred_element_type=jnp.float32,
    )
    return rebuilt.reshape(member_count * own_rows, pod_width).astype(jnp.bfloat16)


def solution(mesh):
    placed = (
        P(("dp", "outer"), "tensor"),
        P(("dp", "outer"), None),
        P(),
        P("tensor", "outer", "dp"),
    )
    return jax.shard_map(
        shards, mesh=mesh, in_specs=placed, out_specs=P("tensor", "outer"), check_vma=False
    )
```

```python
import functools
import math

import jax
import jax.numpy as jnp
from jax import lax
from jax.experimental import pallas as pl
from jax.experimental.pallas import tpu as pltpu
from jax.sharding import PartitionSpec as P

POWER = 2
SIDE = 4
LANES = 128
VMEM_BYTES = 48 * 1024 * 1024

F32 = jnp.float32
BF16 = jnp.bfloat16
NT = (((1,), (1,)), ((), ()))
TN = (((0,), (0,)), ((), ()))


def dot_nt(a, b):
    return lax.dot_general(a, b, NT, preferred_element_type=F32)


def dot_nn(a, b):
    return jnp.dot(a, b, preferred_element_type=F32)


def split2(x):
    high = x.astype(BF16)
    return jnp.concatenate([high, (x - high.astype(F32)).astype(BF16)], axis=0)


def split3(x):
    high = x.astype(BF16)
    rest = x - high.astype(F32)
    middle = rest.astype(BF16)
    low = (rest - middle.astype(F32)).astype(BF16)
    return jnp.concatenate([high, middle, low], axis=0)


def fold(x, times):
    rows = x.shape[0] // times
    total = x[:rows]
    for i in range(1, times):
        total = total + x[i * rows : (i + 1) * rows]
    return total


def orthonormal(left):
    atoms = left.shape[0]
    gram = lax.dot_general(left, left, NT, precision=lax.Precision.HIGHEST, preferred_element_type=F32)
    row = lax.broadcasted_iota(jnp.int32, (atoms, atoms), 0)
    col = lax.broadcasted_iota(jnp.int32, (atoms, atoms), 1)
    diagonal = row == col
    ridge = 1e-05 * jnp.sum(jnp.where(diagonal, gram, 0.0)) / atoms
    gram = gram + jnp.where(diagonal, ridge, 0.0)
    below = lax.broadcasted_iota(jnp.int32, (atoms, 1), 0)
    for j in range(atoms - 1):
        factor = jnp.where(below > j, gram[:, j : j + 1] / gram[j : j + 1, j : j + 1], 0.0)
        left = left - factor * left[j : j + 1]
        gram = gram - factor * gram[j : j + 1]
    pivots = jnp.sum(jnp.where(diagonal, gram, 0.0), axis=1, keepdims=True)
    return left / jnp.sqrt(pivots)


class Ring:
    def __init__(self, place, right, left):
        self.place, self.right, self.left = place, right, left

    def at(self, shift):
        return lax.rem(self.place + shift + SIDE, SIDE)


class Sems:
    def __init__(self, send, recv):
        self.send, self.recv, self.used = send, recv, 0

    def take(self, count):
        first = self.used
        self.used += count
        return first


def chain(
    members,
    atoms,
    own_rows,
    scale,
    h_hbm,
    o_hbm,
    s_hbm,
    kept_ref,
    f2,
    left_out,
    h_v,
    o_v,
    s_v,
    hp,
    o_a,
    o_b,
    zs,
    zr,
    ls,
    lr,
    u_y,
    u_z,
    v_a,
    v_b,
    va_full,
    vb_full,
    w_a,
    w_b,
    rs_v,
    rs_w,
    x_send,
    f1,
    send_sems,
    recv_sems,
    local_sems,
):
    me = lax.axis_index("dp")
    pod = lax.axis_index("outer")
    y, z = lax.rem(me, SIDE), me // SIDE
    ring_y = Ring(y, z * SIDE + lax.rem(y + 1, SIDE), z * SIDE + lax.rem(y + 3, SIDE))
    ring_z = Ring(z, lax.rem(z + 1, SIDE) * SIDE + y, lax.rem(z + 3, SIDE) * SIDE + y)
    tokens, features = o_v.shape
    half = features // 2
    quarter = half // SIDE
    padded = hp.shape[2]
    sems = Sems(send_sems, recv_sems)
    sent = []

    def remote(src, dst, k, dp=None, outer=None):
        device = {"dp": dp} if outer is None else {"outer": outer}
        return pltpu.make_async_remote_copy(
            src_ref=src,
            dst_ref=dst,
            send_sem=sems.send.at[k],
            recv_sem=sems.recv.at[k],
            device_id=device,
            device_id_type=pl.DeviceIdType.MESH,
        )

    def member(shift):
        return lax.rem(me + shift + members, members)

    load_o = pltpu.make_async_copy(o_hbm, o_v, local_sems.at[0])
    load_h = pltpu.make_async_copy(h_hbm, h_v, local_sems.at[1])
    load_s = pltpu.make_async_copy(s_hbm, s_v, local_sems.at[2])
    load_s.start()
    load_o.start()
    load_h.start()
    own_a = pltpu.make_async_copy(
        o_hbm.at[:, pl.ds(pl.multiple_of(y * quarter, quarter), quarter)], o_a.at[y], local_sems.at[3]
    )
    own_b = pltpu.make_async_copy(
        o_hbm.at[:, pl.ds(pl.multiple_of(half + z * quarter, quarter), quarter)], o_b.at[z], local_sems.at[4]
    )
    own_a.start()
    own_b.start()

    barrier = pltpu.get_barrier_semaphore()

    def greet(k, carry):
        pl.semaphore_signal(
            barrier, inc=1, device_id={"dp": member(k)}, device_id_type=pl.DeviceIdType.MESH
        )
        return carry

    lax.fori_loop(1, members, greet, 0)
    pl.semaphore_signal(barrier, inc=1, device_id={"outer": 1 - pod}, device_id_type=pl.DeviceIdType.MESH)
    pl.semaphore_wait(barrier, members)

    regroup = []
    for shift in (1, 3, 2):
        for ring, first, buf, dest in (
            (ring_y, 0, o_a, z * SIDE + ring_y.at(shift)),
            (ring_z, half, o_b, ring_z.at(shift) * SIDE + y),
        ):
            k = sems.take(1)
            begin = pl.multiple_of(first + ring.at(shift) * quarter, quarter)
            copy = remote(o_hbm.at[:, pl.ds(begin, quarter)], buf.at[ring.place], k, dp=dest)
            copy.start()
            sent.append(copy)
            regroup.append(remote(buf.at[ring.at(-shift)], buf.at[ring.at(-shift)], k, dp=dest))

    load_s.wait()
    start3 = split3(s_v[...])
    load_o.wait()
    token_side = dot_nt(start3, o_v[...])
    load_h.wait()
    for e in range(members):
        block = h_v[:, e * own_rows : (e + 1) * own_rows]
        hp[e] = jnp.concatenate([block, jnp.zeros((tokens, padded - own_rows), BF16)], axis=1)
    first3 = split3(fold(token_side, 3))
    for e in range(members):
        zs[0, e] = fold(dot_nn(first3, hp[e]), 3) * scale

    def exchange(src_of, dst, base):
        def go(k, carry):
            to = member(k)
            remote(src_of(to), dst.at[me], base + k, dp=to).start()
            return carry

        def arrive(k, carry):
            came = member(-k)
            remote(dst.at[came], dst.at[came], base + k, dp=came).wait_recv()
            return carry

        lax.fori_loop(1, members, go, 0)
        return lambda: lax.fori_loop(1, members, arrive, 0)

    def sent_exchange(src, base):
        def done(k, carry):
            remote(src, src, base + k, dp=member(k)).wait_send()
            return carry

        lax.fori_loop(1, members, done, 0)

    def gather_start(buf, ring):
        base = sems.take(6)
        rows = buf.shape[1] // 2

        def part(slot, which):
            return buf.at[slot, pl.ds(which * rows, rows)]

        def copy(slot, which, to, k):
            c = remote(part(slot, which), part(slot, which), base + k, dp=to)
            c.start()
            sent.append(c)

        copy(ring.place, 0, ring.right, 0)
        copy(ring.place, 1, ring.left, 2)
        copy(ring.place, 1, ring.right, 1)
        copy(ring.place, 0, ring.left, 3)

        def arrived(slot, which, k):
            remote(part(slot, which), part(slot, which), base + k, dp=ring.right).wait_recv()

        def forward():
            arrived(ring.at(-1), 0, 0)
            copy(ring.at(-1), 0, ring.right, 4)
            arrived(ring.at(1), 1, 2)
            copy(ring.at(1), 1, ring.left, 5)

        def finish():
            arrived(ring.at(-1), 1, 1)
            arrived(ring.at(1), 0, 3)
            arrived(ring.at(2), 0, 4)
            arrived(ring.at(2), 1, 5)

        return forward, finish

    def gather(pairs):
        steps = [gather_start(buf, ring) for buf, ring in pairs]
        for forward, _ in steps:
            forward()
        for _, finish in steps:
            finish()

    def sum_start(parts, land, ring):
        base = sems.take(6)
        rows = parts.shape[1] // 2

        def part(slot, which):
            return parts.at[slot, pl.ds(which * rows, rows)]

        def copy(src, place, to, k):
            c = remote(src, land.at[place], base + k, dp=to)
            c.start()
            sent.append(c)

        copy(part(ring.at(2), 0), 0, ring.right, 0)
        copy(part(ring.at(2), 1), 2, ring.left, 1)
        copy(part(ring.at(1), 1), 1, ring.right, 2)
        copy(part(ring.at(-1), 0), 3, ring.left, 3)

        def arrived(place, k):
            remote(land.at[place], land.at[place], base + k, dp=ring.right).wait_recv()

        def value(slot, which):
            return parts[slot, pl.ds(which * rows, rows)].astype(F32)

        def forward():
            arrived(0, 0)
            land[6] = (land[0].astype(F32) + value(ring.at(1), 0)).astype(BF16)
            copy(land.at[6], 4, ring.right, 4)
            arrived(2, 1)
            land[7] = (land[2].astype(F32) + value(ring.at(-1), 1)).astype(BF16)
            copy(land.at[7], 5, ring.left, 5)

        def finish():
            arrived(1, 2)
            arrived(3, 3)
            arrived(4, 4)
            arrived(5, 5)
            top = value(ring.place, 0) + land[4].astype(F32) + land[3].astype(F32)
            low = value(ring.place, 1) + land[1].astype(F32) + land[5].astype(F32)
            return jnp.concatenate([top, low], axis=0)

        return forward, finish

    def ring_sums(triples):
        steps = [sum_start(*triple) for triple in triples]
        for forward, _ in steps:
            forward()
        return [finish() for _, finish in steps]

    group = members * atoms // SIDE
    for step in range(POWER):
        last = step == POWER - 1
        base = sems.take(members)
        arrive = exchange(lambda i: zs.at[step, i], zr.at[step], base)
        sent_z = base
        zr[step, me] = zs[step, me]
        arrive()
        left = orthonormal(jnp.sum(zr[step], axis=0))
        if last:
            atom = lax.broadcasted_iota(jnp.int32, (atoms, 1), 0)
            left = jnp.where(atom < kept_ref[0, 0], left, 0.0)
        pair = split2(left)
        ls[step] = pair
        lr[step, me] = pair
        base = sems.take(members)
        arrive = exchange(lambda i: ls.at[step], lr.at[step], base)
        arrive()
        sent_exchange(zs.at[step, 0], sent_z)
        sent_exchange(ls.at[step], base)
        if last:
            own_left = pltpu.make_async_copy(
                lr.at[step, :, pl.ds(0, atoms)], left_out.at[:, pod], local_sems.at[5]
            )
            own_left.start()
            left_k = sems.take(1)
            other_left = remote(
                lr.at[step, :, pl.ds(0, atoms)], left_out.at[:, pod], left_k, outer=1 - pod
            )
            other_left.start()
            sent.append(other_left)

        for e in range(members):
            block = (fold(dot_nt(lr[step, e], hp[e]), 2) * scale).astype(BF16)
            u_y[step, y, e * atoms : (e + 1) * atoms] = block
            u_z[step, z, e * atoms : (e + 1) * atoms] = block
        gather([(u_y.at[step], ring_y), (u_z.at[step], ring_z)])

        if step == 0:
            own_a.wait()
            own_b.wait()
            for copy in regroup:
                copy.wait_recv()

        for u, o, v in ((u_y, o_a, v_a), (u_z, o_b, v_b)):
            total = dot_nn(u[step, 0], o[0])
            for c in range(1, SIDE):
                total = total + dot_nn(u[step, c], o[c])
            total = total.astype(BF16)
            for c in range(SIDE):
                v[step, c] = total[c * group : (c + 1) * group]
        sum_a, sum_b = ring_sums(
            [(v_a.at[step], rs_v.at[step, 0], ring_z), (v_b.at[step], rs_v.at[step, 1], ring_y)]
        )
        if last:
            break
        va_full[z] = sum_a.astype(BF16)
        vb_full[y] = sum_b.astype(BF16)
        gather([(va_full, ring_z), (vb_full, ring_y)])
        for v, o, w in ((va_full, o_a, w_a), (vb_full, o_b, w_b)):
            whole = v[...].reshape(members * atoms, quarter)
            for c in range(SIDE):
                w[c] = dot_nt(whole, o[c]).astype(BF16)
        sum_a, sum_b = ring_sums([(w_a, rs_w.at[0], ring_y), (w_b, rs_w.at[1], ring_z)])
        token_side = sum_a + sum_b
        for e in range(members):
            pair = split2(token_side[e * atoms : (e + 1) * atoms])
            zs[step + 1, e] = fold(dot_nn(pair, hp[e]), 2) * scale

    per_row = group // atoms
    mine = jnp.where(pod == 0, sum_a, sum_b).astype(BF16).reshape(per_row, atoms, quarter)
    other = jnp.where(pod == 0, sum_b, sum_a).astype(BF16).reshape(per_row, atoms, quarter)
    row_place = z + pod * (y - z)
    col_place = y + pod * (z - y)
    rows_ring = Ring(
        row_place,
        ring_z.right + pod * (ring_y.right - ring_z.right),
        ring_z.left + pod * (ring_y.left - ring_z.left),
    )
    cols_ring = Ring(
        col_place,
        ring_y.right + pod * (ring_z.right - ring_y.right),
        ring_y.left + pod * (ring_z.left - ring_y.left),
    )
    x_send[...] = other
    k = sems.take(1)
    cross = remote(x_send, f1.at[col_place, :, pod], k, outer=1 - pod)
    cross.start()
    sent.append(cross)
    f1[row_place, :, pod] = mine
    remote(f1.at[row_place, :, 1 - pod], f1.at[row_place, :, 1 - pod], k, outer=1 - pod).wait_recv()
    gather([(f1, rows_ring)])
    own_cols = pltpu.make_async_copy(f1, f2.at[col_place], local_sems.at[6])
    own_cols.start()
    own_cols.wait()
    gather([(f2, cols_ring)])
    own_left.wait()
    other_left.wait_recv()
    for copy in sent:
        copy.wait_send()


def rebuild_kernel(left_ref, right_ref, out_ref):
    own_rows = out_ref.shape[0]
    left = left_ref[0].reshape(-1, left_ref.shape[-1])[:, :own_rows]
    width = right_ref.shape[-1]
    for c in range(right_ref.shape[0]):
        right = right_ref[c, 0].reshape(left.shape[0], width)
        out_ref[:, c * width : (c + 1) * width] = lax.dot_general(
            left, right, TN, preferred_element_type=F32
        ).astype(BF16)


def shards(hidden_act, out_grad, start_vectors, kept_counts):
    tokens, features = out_grad.shape
    atoms = start_vectors.shape[0]
    members = lax.axis_size("dp")
    pods = lax.axis_size("outer")
    hidden_rows = hidden_act.shape[1]
    own_rows = hidden_rows // members
    padded = -(-own_rows // LANES) * LANES
    quarter = features // 2 // SIDE
    group = members * atoms // SIDE
    per_row = group // atoms
    scale = 1.0 / math.sqrt(tokens * members)
    any_space = pl.BlockSpec(memory_space=pl.ANY)
    sem_count = 6 + 4 * members + 2 + 6 * 14
    right_atoms, left_atoms = pl.pallas_call(
        functools.partial(chain, members, atoms, own_rows, scale),
        out_shape=(
            jax.ShapeDtypeStruct((SIDE, SIDE, per_row, pods, atoms, quarter), BF16),
            jax.ShapeDtypeStruct((members, pods, atoms, padded), BF16),
        ),
        in_specs=[any_space, any_space, any_space, pl.BlockSpec(memory_space=pltpu.SMEM)],
        out_specs=(any_space, any_space),
        scratch_shapes=[
            pltpu.VMEM((tokens, hidden_rows), BF16),
            pltpu.VMEM((tokens, features), BF16),
            pltpu.VMEM((atoms, features), F32),
            pltpu.VMEM((members, tokens, padded), BF16),
            pltpu.VMEM((SIDE, tokens, quarter), BF16),
            pltpu.VMEM((SIDE, tokens, quarter), BF16),
            pltpu.VMEM((POWER, members, atoms, padded), F32),
            pltpu.VMEM((POWER, members, atoms, padded), F32),
            pltpu.VMEM((POWER, 2 * atoms, padded), BF16),
            pltpu.VMEM((POWER, members, 2 * atoms, padded), BF16),
            pltpu.VMEM((POWER, SIDE, members * atoms, tokens), BF16),
            pltpu.VMEM((POWER, SIDE, members * atoms, tokens), BF16),
            pltpu.VMEM((POWER, SIDE, group, quarter), BF16),
            pltpu.VMEM((POWER, SIDE, group, quarter), BF16),
            pltpu.VMEM((SIDE, group, quarter), BF16),
            pltpu.VMEM((SIDE, group, quarter), BF16),
            pltpu.VMEM((SIDE, members * atoms, tokens), BF16),
            pltpu.VMEM((SIDE, members * atoms, tokens), BF16),
            pltpu.VMEM((POWER, 2, 8, group // 2, quarter), BF16),
            pltpu.VMEM((2, 8, members * atoms // 2, tokens), BF16),
            pltpu.VMEM((per_row, atoms, quarter), BF16),
            pltpu.VMEM((SIDE, per_row, pods, atoms, quarter), BF16),
            pltpu.SemaphoreType.DMA((sem_count,)),
            pltpu.SemaphoreType.DMA((sem_count,)),
            pltpu.SemaphoreType.DMA((7,)),
        ],
        compiler_params=pltpu.CompilerParams(
            collective_id=0, has_side_effects=True, vmem_limit_bytes=VMEM_BYTES
        ),
        name="power_chain",
    )(hidden_act, out_grad, start_vectors, kept_counts.reshape(1, 1))
    return pl.pallas_call(
        rebuild_kernel,
        out_shape=jax.ShapeDtypeStruct((hidden_rows, features // pods), BF16),
        grid=(members,),
        in_specs=[
            pl.BlockSpec((1, pods, atoms, padded), lambda e: (e, 0, 0, 0)),
            pl.BlockSpec((SIDE, 1, pods, atoms, quarter), lambda e: (0, e, 0, 0, 0)),
        ],
        out_specs=pl.BlockSpec((own_rows, features // pods), lambda e: (e, 0)),
        compiler_params=pltpu.CompilerParams(vmem_limit_bytes=VMEM_BYTES),
        name="rebuild",
    )(left_atoms, right_atoms.reshape(SIDE, members, pods, atoms, quarter))


def solution(mesh):
    placed = (
        P(("dp", "outer"), "tensor"),
        P(("dp", "outer"), None),
        P(),
        P("tensor", "outer", "dp"),
    )
    return jax.shard_map(
        shards, mesh=mesh, in_specs=placed, out_specs=P("tensor", "outer"), check_vma=False
    )
```

```python
import functools
import math

import jax
import jax.numpy as jnp
from jax import lax
from jax.experimental import pallas as pl
from jax.experimental.pallas import tpu as pltpu
from jax.sharding import PartitionSpec as P

POWER = 2
SIDE = 4
LANES = 128
GROUPS = 2
CHUNKS = 8
ROUNDS = (2, 2, 2, 2)
CUT = None
VMEM_BYTES = 60 * 1024 * 1024

F32 = jnp.float32
BF16 = jnp.bfloat16
NT = (((1,), (1,)), ((), ()))
TN = (((0,), (0,)), ((), ()))


def dot_nt(a, b):
    return lax.dot_general(a, b, NT, preferred_element_type=F32)


def dot_nn(a, b):
    return jnp.dot(a, b, preferred_element_type=F32)


def split2(x):
    high = x.astype(BF16)
    return jnp.concatenate([high, (x - high.astype(F32)).astype(BF16)], axis=0)


def split3(x):
    high = x.astype(BF16)
    rest = x - high.astype(F32)
    middle = rest.astype(BF16)
    low = (rest - middle.astype(F32)).astype(BF16)
    return jnp.concatenate([high, middle, low], axis=0)


def fold(x, times):
    rows = x.shape[0] // times
    total = x[:rows]
    for i in range(1, times):
        total = total + x[i * rows : (i + 1) * rows]
    return total


def orthonormal(left):
    atoms = left.shape[0]
    gram = lax.dot_general(left, left, NT, precision=lax.Precision.HIGHEST, preferred_element_type=F32)
    row = lax.broadcasted_iota(jnp.int32, (atoms, atoms), 0)
    col = lax.broadcasted_iota(jnp.int32, (atoms, atoms), 1)
    diagonal = row == col
    ridge = 1e-05 * jnp.sum(jnp.where(diagonal, gram, 0.0)) / atoms
    gram = gram + jnp.where(diagonal, ridge, 0.0)
    below = lax.broadcasted_iota(jnp.int32, (atoms, 1), 0)
    for j in range(atoms - 1):
        factor = jnp.where(below > j, gram[:, j : j + 1] / gram[j : j + 1, j : j + 1], 0.0)
        left = left - factor * left[j : j + 1]
        gram = gram - factor * gram[j : j + 1]
    pivots = jnp.sum(jnp.where(diagonal, gram, 0.0), axis=1, keepdims=True)
    return left / jnp.sqrt(pivots)


class Ring:
    def __init__(self, place, member):
        self.place, self.member = place, member

    def at(self, shift):
        return lax.rem(self.place + shift + SIDE, SIDE)

    def peer(self, shift):
        return self.member(self.at(shift))


SHIFTS = (1, 3, 2)


def chain(
    members,
    atoms,
    own_rows,
    scale,
    h_hbm,
    o_hbm,
    s_hbm,
    kept_ref,
    f2,
    left_out,
    h_v,
    o_v,
    s_v,
    hp,
    o_a,
    o_b,
    zs,
    zr,
    ls,
    lr,
    u_y,
    u_z,
    v_a,
    v_b,
    va_full,
    vb_full,
    w_a,
    w_b,
    rs_v,
    rs_w,
    f1,
    send_sems,
    recv_sems,
    local_sems,
):
    me = lax.axis_index("dp")
    pod = lax.axis_index("outer")
    y, z = lax.rem(me, SIDE), me // SIDE
    ring_y = Ring(y, lambda i: z * SIDE + i)
    ring_z = Ring(z, lambda i: i * SIDE + y)
    rows_ring = Ring(z + pod * (y - z), lambda i: (1 - pod) * (i * SIDE + y) + pod * (z * SIDE + i))
    cols_ring = Ring(y + pod * (z - y), lambda i: (1 - pod) * (z * SIDE + i) + pod * (i * SIDE + y))
    tokens, features = o_v.shape
    half = features // 2
    quarter = half // SIDE
    padded = hp.shape[2]
    share = members // GROUPS
    left_over = []
    taken = [0]

    def take(count):
        taken[0] += count
        return taken[0] - count

    def remote(src, dst, k, recv=None, **device):
        return pltpu.make_async_remote_copy(
            src_ref=src,
            dst_ref=dst,
            send_sem=send_sems.at[k],
            recv_sem=recv_sems.at[k if recv is None else recv],
            device_id=device,
            device_id_type=pl.DeviceIdType.MESH,
        )

    def send(src, dst, k, recv=None, **device):
        copy = remote(src, dst, k, recv, **device)
        copy.start()
        left_over.append(copy.wait_send)

    def came(dst, k, **device):
        remote(dst, dst, k, **device).wait_recv()

    def member(shift):
        return lax.rem(me + shift + members, members)

    load_o = pltpu.make_async_copy(o_hbm, o_v, local_sems.at[0])
    load_h = pltpu.make_async_copy(h_hbm, h_v, local_sems.at[1])
    load_s = pltpu.make_async_copy(s_hbm, s_v, local_sems.at[2])
    load_s.start()
    load_o.start()
    load_h.start()

    barrier = pltpu.get_barrier_semaphore()

    def greet(**device):
        pl.semaphore_signal(barrier, inc=1, device_id=device, device_id_type=pl.DeviceIdType.MESH)

    def greet_member(k, carry):
        greet(dp=member(k))
        return carry

    lax.fori_loop(1, members, greet_member, 0)
    greet(outer=1 - pod)
    for shift in SHIFTS:
        greet(dp=ring_y.peer(shift), outer=1 - pod)
        greet(dp=ring_z.peer(shift), outer=1 - pod)
    load_s.wait()
    start3 = split3(s_v[...])
    load_o.wait()
    pl.semaphore_wait(barrier, members + 2 * len(SHIFTS))

    regroup_base = take(2 * len(SHIFTS))
    plan = [
        (regroup_base + 2 * i + j, shift, ring, first, buf)
        for i, shift in enumerate(SHIFTS)
        for j, (ring, first, buf) in enumerate(((ring_y, 0, o_a), (ring_z, half, o_b)))
    ]
    rounds = [0]

    def regroup_rounds(count):
        rows = tokens // CHUNKS
        for r in range(rounds[0], min(rounds[0] + count, CHUNKS)):
            for k, shift, ring, first, buf in plan:
                begin = pl.multiple_of(first + ring.at(shift) * quarter, quarter)
                remote(
                    o_v.at[pl.ds(r * rows, rows), pl.ds(begin, quarter)],
                    buf.at[ring.place, pl.ds(r * rows, rows)],
                    k,
                    dp=ring.peer(shift),
                ).start()
        rounds[0] = min(rounds[0] + count, CHUNKS)

    def regroup_wait():
        if rounds[0] is None:
            return
        regroup_rounds(CHUNKS)
        rounds[0] = None
        for k, shift, ring, first, buf in plan:
            came(buf.at[ring.at(-shift)], k, dp=ring.peer(shift))
            left_over.append(
                remote(buf.at[ring.place], buf.at[ring.place], k, dp=ring.peer(shift)).wait_send
            )
        own_a.wait()
        own_b.wait()

    regroup_rounds(ROUNDS[0])
    own_a = pltpu.make_async_copy(
        o_v.at[:, pl.ds(pl.multiple_of(y * quarter, quarter), quarter)], o_a.at[y], local_sems.at[3]
    )
    own_b = pltpu.make_async_copy(
        o_v.at[:, pl.ds(pl.multiple_of(half + z * quarter, quarter), quarter)], o_b.at[z], local_sems.at[4]
    )
    own_a.start()
    own_b.start()

    first3 = split3(fold(dot_nt(start3, o_v[...]), 3))
    load_h.wait()

    def ring_gather(buf_of, ring):
        base = take(len(SHIFTS))
        own = buf_of(ring.place)
        for i, shift in enumerate(SHIFTS):
            send(own, own, base + i, dp=ring.peer(shift))

        def wait():
            for i, shift in enumerate(SHIFTS):
                came(buf_of(ring.at(-shift)), base + i, dp=ring.peer(shift))

        return wait

    def ring_sum(parts, land, ring):
        base = take(len(SHIFTS))
        for i, shift in enumerate(SHIFTS):
            send(parts.at[ring.at(shift)], land.at[i], base + i, dp=ring.peer(shift))

        def wait():
            for i, shift in enumerate(SHIFTS):
                came(land.at[i], base + i, dp=ring.peer(shift))

        def total():
            value = parts[ring.place].astype(F32)
            for i in range(len(SHIFTS)):
                value = value + land[i].astype(F32)
            return value

        return wait, total

    def both(*waits):
        def wait():
            for one in waits:
                one()

        return wait

    def piece_chain(g):
        owner = me // share == g
        first = g * share
        rows = slice(first * atoms, (first + share) * atoms)

        def fellow(k):
            return first + lax.rem(lax.rem(me, share) + k, share)

        def each_fellow(do):
            def loop(k, carry):
                do(k)
                return carry

            lax.fori_loop(1, share, loop, 0)
            pl.when(jnp.logical_not(owner))(lambda: do(0))

        def each_member(do):
            def loop(k, carry):
                do(k)
                return carry

            lax.fori_loop(1, members, loop, 0)

        for e in range(first, first + share):
            block = h_v[:, e * own_rows : (e + 1) * own_rows]
            hp[e] = jnp.concatenate([block, jnp.zeros((tokens, padded - own_rows), BF16)], axis=1)
            zs[0, e] = fold(dot_nn(first3, hp[e]), 3) * scale

        for step in range(POWER):
            last = step == POWER - 1
            z_base = take(members)

            def z_copy(k, step=step, z_base=z_base):
                to = fellow(k)
                return remote(zs.at[step, to], zr.at[step, me], z_base + k, z_base + me, dp=to)

            each_fellow(lambda k: z_copy(k).start())
            left_over.append(lambda z_copy=z_copy: each_fellow(lambda k: z_copy(k).wait_send()))

            def z_wait():
                def arrive(k):
                    source = member(k)
                    came(zr.at[step, source], z_base + source, dp=source)

                pl.when(owner)(lambda: each_member(arrive))

            yield z_wait

            left_base = take(members)

            def left_copy(k, step=step, left_base=left_base):
                to = member(k)
                return remote(
                    ls.at[step], lr.at[step, me], left_base + k, left_base + lax.rem(me, share), dp=to
                )

            @pl.when(owner)
            def _():
                zr[step, me] = zs[step, me]
                left = orthonormal(jnp.sum(zr[step], axis=0))
                if last:
                    atom = lax.broadcasted_iota(jnp.int32, (atoms, 1), 0)
                    left = jnp.where(atom < kept_ref[0, 0], left, 0.0)
                pair = split2(left)
                ls[step] = pair
                lr[step, me] = pair
                each_member(lambda k: left_copy(k).start())

            def left_sent(left_copy=left_copy):
                pl.when(owner)(lambda: each_member(lambda k: left_copy(k).wait_send()))

            left_over.append(left_sent)

            def left_wait():
                def arrive(k):
                    source = fellow(k)
                    came(lr.at[step, source], left_base + lax.rem(source, share), dp=source)

                each_fellow(arrive)

            yield left_wait

            for e in range(first, first + share):
                block = (fold(dot_nt(lr[step, e], hp[e]), 2) * scale).astype(BF16)
                u_y[step, y, e * atoms : (e + 1) * atoms] = block
                u_z[step, z, e * atoms : (e + 1) * atoms] = block
            group_rows = pl.ds(first * atoms, share * atoms)
            waits = both(
                ring_gather(lambda i: u_y.at[step, i, group_rows], ring_y),
                ring_gather(lambda i: u_z.at[step, i, group_rows], ring_z),
            )
            if last:
                own_left = pltpu.make_async_copy(
                    lr.at[step, pl.ds(first, share), pl.ds(0, atoms)],
                    left_out.at[pl.ds(first, share), pod],
                    local_sems.at[5 + g],
                )
                own_left.start()
                left_over.append(own_left.wait)
                k = take(1)
                send(
                    lr.at[step, pl.ds(first, share), pl.ds(0, atoms)],
                    left_out.at[pl.ds(first, share), pod],
                    k,
                    outer=1 - pod,
                )
                other_left = left_out.at[pl.ds(first, share), 1 - pod]
                left_over.append(lambda k=k, ref=other_left: came(ref, k, outer=1 - pod))
            yield waits

            regroup_wait()
            for u, o, v in ((u_y, o_a, v_a), (u_z, o_b, v_b)):
                total = dot_nn(u[step, 0, rows], o[0])
                for c in range(1, SIDE):
                    total = total + dot_nn(u[step, c, rows], o[c])
                v[step, g] = total.astype(BF16).reshape(v.shape[2:])
            wait_a, total_a = ring_sum(v_a.at[step, g], rs_v.at[step, g, 0], ring_z)
            wait_b, total_b = ring_sum(v_b.at[step, g], rs_v.at[step, g, 1], ring_y)
            yield both(wait_a, wait_b)
            if last:
                break
            va_full[g, z] = total_a().astype(BF16)
            vb_full[g, y] = total_b().astype(BF16)
            yield both(
                ring_gather(lambda i: va_full.at[g, i], ring_z),
                ring_gather(lambda i: vb_full.at[g, i], ring_y),
            )
            for v, o, w in ((va_full, o_a, w_a), (vb_full, o_b, w_b)):
                whole = v[g].reshape(share * atoms, quarter)
                for c in range(SIDE):
                    w[g, c] = dot_nt(whole, o[c]).astype(BF16)
            wait_a, total_a = ring_sum(w_a.at[g], rs_w.at[g, 0], ring_y)
            wait_b, total_b = ring_sum(w_b.at[g], rs_w.at[g, 1], ring_z)
            yield both(wait_a, wait_b)
            token_side = total_a() + total_b()
            for i in range(share):
                pair = split2(token_side[i * atoms : (i + 1) * atoms])
                zs[step + 1, first + i] = fold(dot_nn(pair, hp[first + i]), 2) * scale

        per_row = share // SIDE
        f1[g, 0] = total_a().astype(BF16).reshape(per_row, atoms, quarter)
        f1[g, 1] = total_b().astype(BF16).reshape(per_row, atoms, quarter)
        row, col = rows_ring.place, cols_ring.place
        base = take(7)
        for i, shift in enumerate(SHIFTS):
            at = base + 2 * i + pod
            send(f1.at[g, 0], f2.at[y, g, z, :, pod], base + i, at, dp=ring_z.peer(shift), outer=0)
            send(f1.at[g, 1], f2.at[z, g, y, :, pod], base + 3 + i, at, dp=ring_y.peer(shift), outer=1)
        send(f1.at[g, 1 - pod], f2.at[row, g, col, :, pod], base + 6, outer=1 - pod)
        keep = pltpu.make_async_copy(f1.at[g, pod], f2.at[col, g, row, :, pod], local_sems.at[5 + GROUPS + g])
        keep.start()

        def own_wait():
            keep.wait()
            came(f2.at[col, g, row, :, 1 - pod], base + 6, outer=1 - pod)

        yield own_wait

        units = []

        def unit_start(slot):
            k = take(6)

            def ref(place, which):
                return f2.at[place, g, slot, :, which]

            def go(shift, which, to, i):
                r = ref(cols_ring.at(shift), which)
                send(r, r, k + i, dp=cols_ring.peer(to))

            def arrived(shift, which, i):
                came(ref(cols_ring.at(shift), which), k + i, dp=cols_ring.peer(1))

            go(0, 0, 1, 0)
            go(0, 1, -1, 2)
            go(0, 1, 1, 1)
            go(0, 0, -1, 3)

            def forward():
                arrived(-1, 0, 0)
                go(-1, 0, 1, 4)
                arrived(1, 1, 2)
                go(1, 1, -1, 5)

            def finish():
                arrived(-1, 1, 1)
                arrived(1, 0, 3)
                arrived(2, 0, 4)
                arrived(2, 1, 5)

            units.append((forward, finish))

        unit_start(row)
        for i, shift in enumerate(SHIFTS):
            slot = rows_ring.at(-shift)

            def row_wait():
                for q in range(2):
                    came(f2.at[col, g, slot, :, q], base + 2 * i + q, dp=rows_ring.peer(shift))

            yield row_wait
            unit_start(slot)
            units[i][0]()
        yield units[-1][0]
        for forward, finish in units:
            finish()

    chains = [piece_chain(g) for g in range(GROUPS)]
    waits = [lambda: None] * GROUPS
    cycle = 0
    while any(wait is not None for wait in waits):
        for g in range(GROUPS):
            if waits[g] is not None:
                waits[g]()
                waits[g] = next(chains[g], None)
        cycle += 1
        if cycle < len(ROUNDS):
            regroup_rounds(ROUNDS[cycle])
        if cycle == CUT:
            for wait in waits:
                wait()
            regroup_wait()
            break
    for wait in left_over:
        wait()


def rebuild_kernel(left_hbm, right_hbm, out_hbm, left_v, right_v, out_v, sems):
    pieces, own_rows, _ = out_v.shape
    width = right_v.shape[-1]
    load_left = pltpu.make_async_copy(left_hbm, left_v, sems.at[2 * pieces])
    load_left.start()
    loads = [pltpu.make_async_copy(right_hbm.at[:, e], right_v.at[:, e], sems.at[e]) for e in range(pieces)]
    stores = [
        pltpu.make_async_copy(out_v.at[e], out_hbm.at[pl.ds(e * own_rows, own_rows)], sems.at[pieces + e])
        for e in range(pieces)
    ]
    for load in loads:
        load.start()
    load_left.wait()
    for e in range(pieces):
        left = left_v[e].reshape(-1, left_v.shape[-1])[:, :own_rows]
        loads[e].wait()
        for c in range(SIDE):
            right = right_v[c, e].reshape(left.shape[0], width)
            out_v[e, :, c * width : (c + 1) * width] = lax.dot_general(
                left, right, TN, preferred_element_type=F32
            ).astype(BF16)
        stores[e].start()
    for store in stores:
        store.wait()


def shards(hidden_act, out_grad, start_vectors, kept_counts):
    tokens, features = out_grad.shape
    atoms = start_vectors.shape[0]
    members = lax.axis_size("dp")
    pods = lax.axis_size("outer")
    hidden_rows = hidden_act.shape[1]
    own_rows = hidden_rows // members
    padded = -(-own_rows // LANES) * LANES
    quarter = features // 2 // SIDE
    share = members // GROUPS
    part = share * atoms // SIDE
    per_row = share // SIDE
    scale = 1.0 / math.sqrt(tokens * members)
    any_space = pl.BlockSpec(memory_space=pl.ANY)
    sem_count = 6 + GROUPS * (POWER * (2 * members + 12) + 12 + 1 + 7 + 24)
    right_atoms, left_atoms = pl.pallas_call(
        functools.partial(chain, members, atoms, own_rows, scale),
        out_shape=(
            jax.ShapeDtypeStruct((SIDE, GROUPS, SIDE, per_row, pods, atoms, quarter), BF16),
            jax.ShapeDtypeStruct((members, pods, atoms, padded), BF16),
        ),
        in_specs=[any_space, any_space, any_space, pl.BlockSpec(memory_space=pltpu.SMEM)],
        out_specs=(any_space, any_space),
        scratch_shapes=[
            pltpu.VMEM((tokens, hidden_rows), BF16),
            pltpu.VMEM((tokens, features), BF16),
            pltpu.VMEM((atoms, features), F32),
            pltpu.VMEM((members, tokens, padded), BF16),
            pltpu.VMEM((SIDE, tokens, quarter), BF16),
            pltpu.VMEM((SIDE, tokens, quarter), BF16),
            pltpu.VMEM((POWER, members, atoms, padded), F32),
            pltpu.VMEM((POWER, members, atoms, padded), F32),
            pltpu.VMEM((POWER, 2 * atoms, padded), BF16),
            pltpu.VMEM((POWER, members, 2 * atoms, padded), BF16),
            pltpu.VMEM((POWER, SIDE, members * atoms, tokens), BF16),
            pltpu.VMEM((POWER, SIDE, members * atoms, tokens), BF16),
            pltpu.VMEM((POWER, GROUPS, SIDE, part, quarter), BF16),
            pltpu.VMEM((POWER, GROUPS, SIDE, part, quarter), BF16),
            pltpu.VMEM((GROUPS, SIDE, part, quarter), BF16),
            pltpu.VMEM((GROUPS, SIDE, part, quarter), BF16),
            pltpu.VMEM((GROUPS, SIDE, share * atoms, tokens), BF16),
            pltpu.VMEM((GROUPS, SIDE, share * atoms, tokens), BF16),
            pltpu.VMEM((POWER, GROUPS, 2, 3, part, quarter), BF16),
            pltpu.VMEM((GROUPS, 2, 3, share * atoms, tokens), BF16),
            pltpu.VMEM((GROUPS, 2, per_row, atoms, quarter), BF16),
            pltpu.SemaphoreType.DMA((sem_count,)),
            pltpu.SemaphoreType.DMA((sem_count,)),
            pltpu.SemaphoreType.DMA((5 + 2 * GROUPS,)),
        ],
        compiler_params=pltpu.CompilerParams(
            collective_id=0, has_side_effects=True, vmem_limit_bytes=VMEM_BYTES
        ),
        name="power_chain",
    )(hidden_act, out_grad, start_vectors, kept_counts.reshape(1, 1))
    return pl.pallas_call(
        rebuild_kernel,
        out_shape=jax.ShapeDtypeStruct((hidden_rows, features // pods), BF16),
        in_specs=[any_space, any_space],
        out_specs=any_space,
        scratch_shapes=[
            pltpu.VMEM((members, pods, atoms, padded), BF16),
            pltpu.VMEM((SIDE, members, pods, atoms, quarter), BF16),
            pltpu.VMEM((members, own_rows, features // pods), BF16),
            pltpu.SemaphoreType.DMA((2 * members + 1,)),
        ],
        compiler_params=pltpu.CompilerParams(vmem_limit_bytes=VMEM_BYTES),
        name="rebuild",
    )(left_atoms, right_atoms.reshape(SIDE, members, pods, atoms, quarter))


def solution(mesh):
    placed = (
        P(("dp", "outer"), "tensor"),
        P(("dp", "outer"), None),
        P(),
        P("tensor", "outer", "dp"),
    )
    return jax.shard_map(
        shards, mesh=mesh, in_specs=placed, out_specs=P("tensor", "outer"), check_vma=False
    )
```

```python
import functools
import math

import jax
import jax.numpy as jnp
from jax import lax
from jax.experimental import pallas as pl
from jax.experimental.pallas import tpu as pltpu
from jax.sharding import PartitionSpec as P

POWER = 2
SIDE = 4
LANES = 128
GROUPS = 2
CHUNKS = 4
ROUNDS = (1, 1, 1, 1)
CUT = None
VMEM_BYTES = 60 * 1024 * 1024

F32 = jnp.float32
BF16 = jnp.bfloat16
NT = (((1,), (1,)), ((), ()))
TN = (((0,), (0,)), ((), ()))


def dot_nt(a, b):
    return lax.dot_general(a, b, NT, preferred_element_type=F32)


def dot_nn(a, b):
    return jnp.dot(a, b, preferred_element_type=F32)


def split2(x):
    high = x.astype(BF16)
    return jnp.concatenate([high, (x - high.astype(F32)).astype(BF16)], axis=0)


def split3(x):
    high = x.astype(BF16)
    rest = x - high.astype(F32)
    middle = rest.astype(BF16)
    low = (rest - middle.astype(F32)).astype(BF16)
    return jnp.concatenate([high, middle, low], axis=0)


def fold(x, times):
    rows = x.shape[0] // times
    total = x[:rows]
    for i in range(1, times):
        total = total + x[i * rows : (i + 1) * rows]
    return total


def orthonormal(left):
    atoms = left.shape[0]
    gram = lax.dot_general(left, left, NT, precision=lax.Precision.HIGHEST, preferred_element_type=F32)
    row = lax.broadcasted_iota(jnp.int32, (atoms, atoms), 0)
    col = lax.broadcasted_iota(jnp.int32, (atoms, atoms), 1)
    diagonal = row == col
    ridge = 1e-05 * jnp.sum(jnp.where(diagonal, gram, 0.0)) / atoms
    gram = gram + jnp.where(diagonal, ridge, 0.0)
    below = lax.broadcasted_iota(jnp.int32, (atoms, 1), 0)
    for j in range(atoms - 1):
        factor = jnp.where(below > j, gram[:, j : j + 1] / gram[j : j + 1, j : j + 1], 0.0)
        left = left - factor * left[j : j + 1]
        gram = gram - factor * gram[j : j + 1]
    pivots = jnp.sum(jnp.where(diagonal, gram, 0.0), axis=1, keepdims=True)
    return left / jnp.sqrt(pivots)


class Ring:
    def __init__(self, place, member):
        self.place, self.member = place, member

    def at(self, shift):
        return lax.rem(self.place + shift + SIDE, SIDE)

    def peer(self, shift):
        return self.member(self.at(shift))


SHIFTS = (1, 3, 2)


def chain(
    members,
    atoms,
    own_rows,
    scale,
    h_hbm,
    o_hbm,
    s_hbm,
    kept_ref,
    right_out,
    left_out,
    h_v,
    o_v,
    s_v,
    hp,
    o_a,
    o_b,
    zs,
    zr,
    ls,
    lr,
    u_y,
    u_z,
    v_a,
    v_b,
    va_full,
    vb_full,
    w_a,
    w_b,
    rs_v,
    rs_w,
    f1,
    f2,
    send_sems,
    recv_sems,
    local_sems,
):
    me = lax.axis_index("dp")
    pod = lax.axis_index("outer")
    y, z = lax.rem(me, SIDE), me // SIDE
    ring_y = Ring(y, lambda i: z * SIDE + i)
    ring_z = Ring(z, lambda i: i * SIDE + y)
    rows_ring = Ring(z + pod * (y - z), lambda i: (1 - pod) * (i * SIDE + y) + pod * (z * SIDE + i))
    cols_ring = Ring(y + pod * (z - y), lambda i: (1 - pod) * (z * SIDE + i) + pod * (i * SIDE + y))
    tokens, features = o_v.shape
    half = features // 2
    quarter = half // SIDE
    padded = hp.shape[2]
    share = members // GROUPS
    left_over = []
    taken = [0]

    def take(count):
        taken[0] += count
        return taken[0] - count

    def remote(src, dst, k, recv=None, **device):
        return pltpu.make_async_remote_copy(
            src_ref=src,
            dst_ref=dst,
            send_sem=send_sems.at[k],
            recv_sem=recv_sems.at[k if recv is None else recv],
            device_id=device,
            device_id_type=pl.DeviceIdType.MESH,
        )

    def send(src, dst, k, recv=None, **device):
        remote(src, dst, k, recv, **device).start()

    def came(dst, k):
        remote(dst, dst, k, outer=1 - pod).wait_recv()

    def went(src, k):
        left_over.append(lambda: remote(src, src, k, outer=1 - pod).wait_send())

    def member(shift):
        return lax.rem(me + shift + members, members)

    load_o = pltpu.make_async_copy(o_hbm, o_v, local_sems.at[0])
    load_h = pltpu.make_async_copy(h_hbm, h_v, local_sems.at[1])
    load_s = pltpu.make_async_copy(s_hbm, s_v, local_sems.at[2])
    load_s.start()
    load_o.start()
    load_h.start()

    barrier = pltpu.get_barrier_semaphore()

    def greet(**device):
        pl.semaphore_signal(barrier, inc=1, device_id=device, device_id_type=pl.DeviceIdType.MESH)

    def greet_member(k, carry):
        greet(dp=member(k))
        return carry

    lax.fori_loop(1, members, greet_member, 0)
    greet(outer=1 - pod)
    for shift in SHIFTS:
        greet(dp=ring_y.peer(shift), outer=1 - pod)
        greet(dp=ring_z.peer(shift), outer=1 - pod)
    load_s.wait()
    start3 = split3(s_v[...])
    load_o.wait()
    pl.semaphore_wait(barrier, members + 2 * len(SHIFTS))

    regroup_base = take(2 * len(SHIFTS))
    plan = [
        (regroup_base + 2 * i + j, shift, ring, first, buf)
        for i, shift in enumerate(SHIFTS)
        for j, (ring, first, buf) in enumerate(((ring_y, 0, o_a), (ring_z, half, o_b)))
    ]
    rounds = [0]

    def regroup_rounds(count):
        rows = tokens // CHUNKS
        for r in range(rounds[0], min(rounds[0] + count, CHUNKS)):
            for k, shift, ring, first, buf in plan:
                begin = pl.multiple_of(first + ring.at(shift) * quarter, quarter)
                remote(
                    o_v.at[pl.ds(r * rows, rows), pl.ds(begin, quarter)],
                    buf.at[ring.place, pl.ds(r * rows, rows)],
                    k,
                    dp=ring.peer(shift),
                ).start()
        rounds[0] = min(rounds[0] + count, CHUNKS)

    def regroup_wait():
        if rounds[0] is None:
            return
        regroup_rounds(CHUNKS)
        rounds[0] = None
        for k, shift, ring, first, buf in plan:
            came(buf.at[ring.at(-shift)], k)
            went(buf.at[ring.place], k)
        own_a.wait()
        own_b.wait()

    regroup_rounds(ROUNDS[0])
    own_a = pltpu.make_async_copy(
        o_v.at[:, pl.ds(pl.multiple_of(y * quarter, quarter), quarter)], o_a.at[y], local_sems.at[3]
    )
    own_b = pltpu.make_async_copy(
        o_v.at[:, pl.ds(pl.multiple_of(half + z * quarter, quarter), quarter)], o_b.at[z], local_sems.at[4]
    )
    own_a.start()
    own_b.start()

    first3 = split3(fold(dot_nt(start3, o_v[...]), 3))
    load_h.wait()

    def ring_gather(buf, ring):
        k = take(1)
        own = buf(ring.place)
        for shift in SHIFTS:
            send(own, own, k, dp=ring.peer(shift))
        three = buf(pl.ds(0, len(SHIFTS)))
        went(three, k)
        return lambda: came(three, k)

    def ring_sum(parts, land, ring):
        k = take(1)
        for i, shift in enumerate(SHIFTS):
            send(parts.at[ring.at(shift)], land.at[i], k, dp=ring.peer(shift))
        went(land, k)

        def wait():
            came(land, k)

        def total():
            value = parts[ring.place].astype(F32)
            for i in range(len(SHIFTS)):
                value = value + land[i].astype(F32)
            return value

        return wait, total

    def both(*waits):
        def wait():
            for one in waits:
                one()

        return wait

    def piece_chain(g):
        owner = me // share == g
        first = g * share
        rows = slice(first * atoms, (first + share) * atoms)

        def fellow(k):
            return first + lax.rem(lax.rem(me, share) + k, share)

        def each_fellow(do):
            def loop(k, carry):
                do(k)
                return carry

            lax.fori_loop(1, share, loop, 0)
            pl.when(jnp.logical_not(owner))(lambda: do(0))

        def by_owner(wait, call=lambda f: f()):
            call(lambda: pl.when(owner)(lambda: wait(share - 1)))
            call(lambda: pl.when(jnp.logical_not(owner))(lambda: wait(share)))

        def each_member(do):
            def loop(k, carry):
                do(k)
                return carry

            lax.fori_loop(1, members, loop, 0)

        for e in range(first, first + share):
            block = h_v[:, e * own_rows : (e + 1) * own_rows]
            hp[e] = jnp.concatenate([block, jnp.zeros((tokens, padded - own_rows), BF16)], axis=1)
            zs[0, e] = (fold(dot_nn(first3, hp[e]), 3) * scale).astype(BF16)

        for step in range(POWER):
            last = step == POWER - 1
            z_k = take(1)

            def z_send(k):
                to = fellow(k)
                send(zs.at[step, to], zr.at[step, me], z_k, dp=to)

            each_fellow(z_send)
            by_owner(
                lambda count, step=step, z_k=z_k: remote(
                    zs.at[step, pl.ds(0, count)], zs.at[step, pl.ds(0, count)], z_k, outer=1 - pod
                ).wait_send(),
                left_over.append,
            )

            def z_wait():
                pl.when(owner)(lambda: came(zr.at[step, pl.ds(0, members - 1)], z_k))

            yield z_wait

            left_k = take(2)

            @pl.when(owner)
            def _():
                zr[step, me] = zs[step, me]
                left = orthonormal(jnp.sum(zr[step].astype(F32), axis=0))
                if last:
                    atom = lax.broadcasted_iota(jnp.int32, (atoms, 1), 0)
                    left = jnp.where(atom < kept_ref[0, 0], left, 0.0)
                rounded = left.astype(BF16)
                ls[step] = rounded
                lr[step, me] = rounded

                def left_send(k):
                    send(ls.at[step], lr.at[step, me], left_k, left_k + 1, dp=member(k))

                each_member(left_send)

            def left_sent(step=step, left_k=left_k):
                all_sent = lr.at[step, pl.ds(0, members - 1)]
                pl.when(owner)(lambda: remote(all_sent, all_sent, left_k, outer=1 - pod).wait_send())

            left_over.append(left_sent)

            def left_wait():
                by_owner(lambda count: came(lr.at[step, pl.ds(first, count)], left_k + 1))

            yield left_wait

            for e in range(first, first + share):
                block = (dot_nt(lr[step, e], hp[e]) * scale).astype(BF16)
                u_y[step, y, e * atoms : (e + 1) * atoms] = block
                u_z[step, z, e * atoms : (e + 1) * atoms] = block
            group_rows = pl.ds(first * atoms, share * atoms)
            waits = both(
                ring_gather(lambda i: u_y.at[step, i, group_rows], ring_y),
                ring_gather(lambda i: u_z.at[step, i, group_rows], ring_z),
            )
            if last:
                own_left = pltpu.make_async_copy(
                    lr.at[step, pl.ds(first, share)],
                    left_out.at[pl.ds(first, share), pod],
                    local_sems.at[5 + g],
                )
                own_left.start()
                left_over.append(own_left.wait)
                k = take(1)
                send(
                    lr.at[step, pl.ds(first, share)],
                    left_out.at[pl.ds(first, share), pod],
                    k,
                    outer=1 - pod,
                )
                other_left = left_out.at[pl.ds(first, share), 1 - pod]
                went(other_left, k)
                left_over.append(lambda k=k, ref=other_left: came(ref, k))
            yield waits

            regroup_wait()
            for u, o, v in ((u_y, o_a, v_a), (u_z, o_b, v_b)):
                total = dot_nn(u[step, 0, rows], o[0])
                for c in range(1, SIDE):
                    total = total + dot_nn(u[step, c, rows], o[c])
                v[step, g] = total.astype(BF16).reshape(v.shape[2:])
            wait_a, total_a = ring_sum(v_a.at[step, g], rs_v.at[step, g, 0], ring_z)
            wait_b, total_b = ring_sum(v_b.at[step, g], rs_v.at[step, g, 1], ring_y)
            yield both(wait_a, wait_b)
            if last:
                break
            va_full[g, z] = total_a().astype(BF16)
            vb_full[g, y] = total_b().astype(BF16)
            yield both(
                ring_gather(lambda i: va_full.at[g, i], ring_z),
                ring_gather(lambda i: vb_full.at[g, i], ring_y),
            )
            for v, o, w in ((va_full, o_a, w_a), (vb_full, o_b, w_b)):
                whole = v[g].reshape(share * atoms, quarter)
                for c in range(SIDE):
                    w[g, c] = dot_nt(whole, o[c]).astype(BF16)
            wait_a, total_a = ring_sum(w_a.at[g], rs_w.at[g, 0], ring_y)
            wait_b, total_b = ring_sum(w_b.at[g], rs_w.at[g, 1], ring_z)
            yield both(wait_a, wait_b)
            token_side = total_a() + total_b()
            for i in range(share):
                pair = split2(token_side[i * atoms : (i + 1) * atoms])
                zs[step + 1, first + i] = (fold(dot_nn(pair, hp[first + i]), 2) * scale).astype(BF16)

        f1[g, 0] = total_a().astype(BF16).reshape(f1.shape[2:])
        f1[g, 1] = total_b().astype(BF16).reshape(f1.shape[2:])
        for i, shift in enumerate(SHIFTS):
            send(f1.at[g, 0], f2.at[y, z, g, :, pod], row_k, row_k + i, dp=ring_z.peer(shift), outer=0)
            send(f1.at[g, 1], f2.at[z, y, g, :, pod], row_k, row_k + i, dp=ring_y.peer(shift), outer=1)
        send(f1.at[g, 1 - pod], f2.at[row, col, g, :, pod], cross_k, outer=1 - pod)
        f2[col, row, g, :, pod] = f1[g, pod]

    row, col = rows_ring.place, cols_ring.place
    row_k, cross_k, unit_k, far_k = take(len(SHIFTS)), take(1), take(2 * SIDE), take(1)

    chains = [piece_chain(g) for g in range(GROUPS)]
    waits = [lambda: None] * GROUPS
    cycle = 0
    while any(wait is not None for wait in waits):
        for g in range(GROUPS):
            if waits[g] is not None:
                waits[g]()
                waits[g] = next(chains[g], None)
        cycle += 1
        if cycle < len(ROUNDS):
            regroup_rounds(ROUNDS[cycle])
        if cycle == CUT:
            for wait in waits:
                if wait is not None:
                    wait()
            regroup_wait()
            break
    if CUT is None:
        went(f2.at[0, pl.ds(0, 3)], row_k)

        def go(shift, slot, which, to, recv):
            ref = f2.at[cols_ring.at(shift), slot, :, :, which]
            send(ref, ref, far_k, recv, dp=cols_ring.peer(to))

        def unit_start(slot, i):
            go(0, slot, 0, 1, unit_k + 2 * i)
            go(0, slot, 1, -1, unit_k + 2 * i + 1)
            go(0, slot, 1, 1, far_k)
            go(0, slot, 0, -1, far_k)

        def unit_forward(slot, i):
            came(f2.at[cols_ring.at(-1), slot, :, :, 0], unit_k + 2 * i)
            go(-1, slot, 0, 1, far_k)
            came(f2.at[cols_ring.at(1), slot, :, :, 1], unit_k + 2 * i + 1)
            go(1, slot, 1, -1, far_k)

        came(f2.at[col, row, :, :, 1 - pod], cross_k)
        went(f2.at[col, row, :, :, 1 - pod], cross_k)
        unit_start(row, 0)
        slots = [row]
        for i, shift in enumerate(SHIFTS):
            slots.append(rows_ring.at(-shift))
            came(f2.at[col, slots[-1]], row_k + i)
            unit_start(slots[-1], i + 1)
            unit_forward(slots[-2], i)
        unit_forward(slots[-1], SIDE - 1)
        came(f2.at[pl.ds(0, 2)], far_k)
        went(f2.at[pl.ds(0, 3)], far_k)
        out = pltpu.make_async_copy(f2, right_out, local_sems.at[5 + GROUPS])
        out.start()
        left_over.append(out.wait)
    for wait in left_over:
        wait()


def rebuild_kernel(left_hbm, right_hbm, out_hbm, left_v, right_v, out_v, sems):
    pieces, own_rows, _ = out_v.shape
    per_row = pieces // GROUPS // SIDE

    def place(e):
        group, rest = divmod(e, pieces // GROUPS)
        return rest // per_row * (pieces // SIDE) + group * per_row + rest % per_row

    width = right_v.shape[-1]
    load_left = pltpu.make_async_copy(left_hbm, left_v, sems.at[2 * pieces])
    load_left.start()
    loads = [pltpu.make_async_copy(right_hbm.at[:, place(e)], right_v.at[:, e], sems.at[e]) for e in range(pieces)]
    stores = [
        pltpu.make_async_copy(out_v.at[e], out_hbm.at[pl.ds(e * own_rows, own_rows)], sems.at[pieces + e])
        for e in range(pieces)
    ]
    for load in loads:
        load.start()
    load_left.wait()
    for e in range(pieces):
        left = left_v[e].reshape(-1, left_v.shape[-1])[:, :own_rows]
        loads[e].wait()
        for c in range(SIDE):
            right = right_v[c, e].reshape(left.shape[0], width)
            out_v[e, :, c * width : (c + 1) * width] = lax.dot_general(
                left, right, TN, preferred_element_type=F32
            ).astype(BF16)
        stores[e].start()
    for store in stores:
        store.wait()


def shards(hidden_act, out_grad, start_vectors, kept_counts):
    tokens, features = out_grad.shape
    atoms = start_vectors.shape[0]
    members = lax.axis_size("dp")
    pods = lax.axis_size("outer")
    hidden_rows = hidden_act.shape[1]
    own_rows = hidden_rows // members
    padded = -(-own_rows // LANES) * LANES
    quarter = features // 2 // SIDE
    share = members // GROUPS
    part = share * atoms // SIDE
    per_row = share // SIDE
    scale = 1.0 / math.sqrt(tokens * members)
    any_space = pl.BlockSpec(memory_space=pl.ANY)
    sem_count = 6 + GROUPS * (POWER * 7 + 5) + 13
    right_atoms, left_atoms = pl.pallas_call(
        functools.partial(chain, members, atoms, own_rows, scale),
        out_shape=(
            jax.ShapeDtypeStruct((SIDE, SIDE, GROUPS, per_row, pods, atoms, quarter), BF16),
            jax.ShapeDtypeStruct((members, pods, atoms, padded), BF16),
        ),
        in_specs=[any_space, any_space, any_space, pl.BlockSpec(memory_space=pltpu.SMEM)],
        out_specs=(any_space, any_space),
        scratch_shapes=[
            pltpu.VMEM((tokens, hidden_rows), BF16),
            pltpu.VMEM((tokens, features), BF16),
            pltpu.VMEM((atoms, features), F32),
            pltpu.VMEM((members, tokens, padded), BF16),
            pltpu.VMEM((SIDE, tokens, quarter), BF16),
            pltpu.VMEM((SIDE, tokens, quarter), BF16),
            pltpu.VMEM((POWER, members, atoms, padded), BF16),
            pltpu.VMEM((POWER, members, atoms, padded), BF16),
            pltpu.VMEM((POWER, atoms, padded), BF16),
            pltpu.VMEM((POWER, members, atoms, padded), BF16),
            pltpu.VMEM((POWER, SIDE, members * atoms, tokens), BF16),
            pltpu.VMEM((POWER, SIDE, members * atoms, tokens), BF16),
            pltpu.VMEM((POWER, GROUPS, SIDE, part, quarter), BF16),
            pltpu.VMEM((POWER, GROUPS, SIDE, part, quarter), BF16),
            pltpu.VMEM((GROUPS, SIDE, part, quarter), BF16),
            pltpu.VMEM((GROUPS, SIDE, part, quarter), BF16),
            pltpu.VMEM((GROUPS, SIDE, share * atoms, tokens), BF16),
            pltpu.VMEM((GROUPS, SIDE, share * atoms, tokens), BF16),
            pltpu.VMEM((POWER, GROUPS, 2, 3, part, quarter), BF16),
            pltpu.VMEM((GROUPS, 2, 3, share * atoms, tokens), BF16),
            pltpu.VMEM((GROUPS, 2, per_row, atoms, quarter), BF16),
            pltpu.VMEM((SIDE, SIDE, GROUPS, per_row, pods, atoms, quarter), BF16),
            pltpu.SemaphoreType.DMA((sem_count,)),
            pltpu.SemaphoreType.DMA((sem_count,)),
            pltpu.SemaphoreType.DMA((6 + GROUPS,)),
        ],
        compiler_params=pltpu.CompilerParams(
            collective_id=0, has_side_effects=True, vmem_limit_bytes=VMEM_BYTES
        ),
        name="power_chain",
    )(hidden_act, out_grad, start_vectors, kept_counts.reshape(1, 1))
    return pl.pallas_call(
        rebuild_kernel,
        out_shape=jax.ShapeDtypeStruct((hidden_rows, features // pods), BF16),
        in_specs=[any_space, any_space],
        out_specs=any_space,
        scratch_shapes=[
            pltpu.VMEM((members, pods, atoms, padded), BF16),
            pltpu.VMEM((SIDE, members, pods, atoms, quarter), BF16),
            pltpu.VMEM((members, own_rows, features // pods), BF16),
            pltpu.SemaphoreType.DMA((2 * members + 1,)),
        ],
        compiler_params=pltpu.CompilerParams(vmem_limit_bytes=VMEM_BYTES),
        name="rebuild",
    )(left_atoms, right_atoms.reshape(SIDE, members, pods, atoms, quarter))


def solution(mesh):
    placed = (
        P(("dp", "outer"), "tensor"),
        P(("dp", "outer"), None),
        P(),
        P("tensor", "outer", "dp"),
    )
    return jax.shard_map(
        shards, mesh=mesh, in_specs=placed, out_specs=P("tensor", "outer"), check_vma=False
    )
```

```python
import functools
import math

import jax
import jax.numpy as jnp
from jax import lax
from jax.experimental import pallas as pl
from jax.experimental.pallas import tpu as pltpu
from jax.sharding import PartitionSpec as P

POWER = 2
SIDE = 4
LANES = 128
GROUPS = 4
CHUNKS = 4
ROUNDS = (2, 1, 1)
CUT = None
VMEM_BYTES = 60 * 1024 * 1024

F32 = jnp.float32
BF16 = jnp.bfloat16
NT = (((1,), (1,)), ((), ()))
TN = (((0,), (0,)), ((), ()))


def dot_nt(a, b):
    return lax.dot_general(a, b, NT, preferred_element_type=F32)


def dot_nn(a, b):
    return jnp.dot(a, b, preferred_element_type=F32)


def split2(x):
    high = x.astype(BF16)
    return jnp.concatenate([high, (x - high.astype(F32)).astype(BF16)], axis=0)


def split3(x):
    high = x.astype(BF16)
    rest = x - high.astype(F32)
    middle = rest.astype(BF16)
    low = (rest - middle.astype(F32)).astype(BF16)
    return jnp.concatenate([high, middle, low], axis=0)


def fold(x, times):
    rows = x.shape[0] // times
    total = x[:rows]
    for i in range(1, times):
        total = total + x[i * rows : (i + 1) * rows]
    return total


def orthonormal(left):
    atoms = left.shape[0]
    gram = lax.dot_general(left, left, NT, precision=lax.Precision.HIGHEST, preferred_element_type=F32)
    row = lax.broadcasted_iota(jnp.int32, (atoms, atoms), 0)
    col = lax.broadcasted_iota(jnp.int32, (atoms, atoms), 1)
    diagonal = row == col
    ridge = 1e-05 * jnp.sum(jnp.where(diagonal, gram, 0.0)) / atoms
    gram = gram + jnp.where(diagonal, ridge, 0.0)
    below = lax.broadcasted_iota(jnp.int32, (atoms, 1), 0)
    for j in range(atoms - 1):
        factor = jnp.where(below > j, gram[:, j : j + 1] / gram[j : j + 1, j : j + 1], 0.0)
        left = left - factor * left[j : j + 1]
        gram = gram - factor * gram[j : j + 1]
    pivots = jnp.sum(jnp.where(diagonal, gram, 0.0), axis=1, keepdims=True)
    return left / jnp.sqrt(pivots)


class Ring:
    def __init__(self, place, member):
        self.place, self.member = place, member

    def at(self, shift):
        return lax.rem(self.place + shift + SIDE, SIDE)

    def peer(self, shift):
        return self.member(self.at(shift))


SHIFTS = (1, 3, 2)


def chain(
    members,
    atoms,
    own_rows,
    scale,
    h_hbm,
    o_hbm,
    s_hbm,
    kept_ref,
    right_out,
    left_out,
    h_v,
    o_v,
    s_v,
    hp,
    o_a,
    o_b,
    zs,
    zr,
    ls,
    lr,
    u_y,
    u_z,
    v_a,
    v_b,
    va_full,
    vb_full,
    w_a,
    w_b,
    rs_v,
    rs_w,
    f1,
    f2,
    send_sems,
    recv_sems,
    local_sems,
):
    me = lax.axis_index("dp")
    pod = lax.axis_index("outer")
    y, z = lax.rem(me, SIDE), me // SIDE
    ring_y = Ring(y, lambda i: z * SIDE + i)
    ring_z = Ring(z, lambda i: i * SIDE + y)
    rows_ring = Ring(z + pod * (y - z), lambda i: (1 - pod) * (i * SIDE + y) + pod * (z * SIDE + i))
    cols_ring = Ring(y + pod * (z - y), lambda i: (1 - pod) * (z * SIDE + i) + pod * (i * SIDE + y))
    tokens, features = o_v.shape
    half = features // 2
    quarter = half // SIDE
    padded = hp.shape[2]
    share = members // GROUPS
    left_over = []
    taken = [0]

    def take(count):
        taken[0] += count
        return taken[0] - count

    def remote(src, dst, k, recv=None, **device):
        return pltpu.make_async_remote_copy(
            src_ref=src,
            dst_ref=dst,
            send_sem=send_sems.at[k],
            recv_sem=recv_sems.at[k if recv is None else recv],
            device_id=device,
            device_id_type=pl.DeviceIdType.MESH,
        )

    def send(src, dst, k, recv=None, **device):
        remote(src, dst, k, recv, **device).start()

    def came(dst, k):
        remote(dst, dst, k, outer=1 - pod).wait_recv()

    def went(src, k):
        left_over.append(lambda: remote(src, src, k, outer=1 - pod).wait_send())

    def member(shift):
        return lax.rem(me + shift + members, members)

    load_o = pltpu.make_async_copy(o_hbm, o_v, local_sems.at[0])
    load_h = pltpu.make_async_copy(h_hbm, h_v, local_sems.at[1])
    load_s = pltpu.make_async_copy(s_hbm, s_v, local_sems.at[2])
    load_s.start()
    load_o.start()
    load_h.start()

    barrier = pltpu.get_barrier_semaphore()

    def greet(**device):
        pl.semaphore_signal(barrier, inc=1, device_id=device, device_id_type=pl.DeviceIdType.MESH)

    def greet_member(k, carry):
        greet(dp=member(k))
        return carry

    lax.fori_loop(1, members, greet_member, 0)
    greet(outer=1 - pod)
    for shift in SHIFTS:
        greet(dp=ring_y.peer(shift), outer=1 - pod)
        greet(dp=ring_z.peer(shift), outer=1 - pod)
    load_s.wait()
    start3 = split3(s_v[...])
    load_o.wait()
    pl.semaphore_wait(barrier, members + 2 * len(SHIFTS))

    regroup_base = take(2 * len(SHIFTS))
    plan = [
        (regroup_base + 2 * i + j, shift, ring, first, buf)
        for i, shift in enumerate(SHIFTS)
        for j, (ring, first, buf) in enumerate(((ring_y, 0, o_a), (ring_z, half, o_b)))
    ]
    rounds = [0]

    def regroup_rounds(count):
        rows = tokens // CHUNKS
        for r in range(rounds[0], min(rounds[0] + count, CHUNKS)):
            for k, shift, ring, first, buf in plan:
                begin = pl.multiple_of(first + ring.at(shift) * quarter, quarter)
                remote(
                    o_v.at[pl.ds(r * rows, rows), pl.ds(begin, quarter)],
                    buf.at[ring.place, pl.ds(r * rows, rows)],
                    k,
                    dp=ring.peer(shift),
                ).start()
        rounds[0] = min(rounds[0] + count, CHUNKS)

    def regroup_wait():
        if rounds[0] is None:
            return
        regroup_rounds(CHUNKS)
        rounds[0] = None
        for k, shift, ring, first, buf in plan:
            came(buf.at[ring.at(-shift)], k)
            went(buf.at[ring.place], k)
        own_a.wait()
        own_b.wait()

    regroup_rounds(ROUNDS[0])
    own_a = pltpu.make_async_copy(
        o_v.at[:, pl.ds(pl.multiple_of(y * quarter, quarter), quarter)], o_a.at[y], local_sems.at[3]
    )
    own_b = pltpu.make_async_copy(
        o_v.at[:, pl.ds(pl.multiple_of(half + z * quarter, quarter), quarter)], o_b.at[z], local_sems.at[4]
    )
    own_a.start()
    own_b.start()

    first3 = split3(fold(dot_nt(start3, o_v[...]), 3))
    load_h.wait()

    def ring_gather(buf, ring):
        k = take(1)
        own = buf(ring.place)
        for shift in SHIFTS:
            send(own, own, k, dp=ring.peer(shift))
        three = buf(pl.ds(0, len(SHIFTS)))
        went(three, k)
        return lambda: came(three, k)

    def ring_sum(parts, land, ring):
        k = take(1)
        for i, shift in enumerate(SHIFTS):
            send(parts.at[ring.at(shift)], land.at[i], k, dp=ring.peer(shift))
        went(land, k)

        def wait():
            came(land, k)

        def total():
            value = parts[ring.place].astype(F32)
            for i in range(len(SHIFTS)):
                value = value + land[i].astype(F32)
            return value

        return wait, total

    def both(*waits):
        def wait():
            for one in waits:
                one()

        return wait

    def piece_chain(g):
        owner = me // share == g
        first = g * share
        rows = slice(first * atoms, (first + share) * atoms)

        def fellow(k):
            return first + lax.rem(lax.rem(me, share) + k, share)

        def each_fellow(do):
            def loop(k, carry):
                do(k)
                return carry

            lax.fori_loop(1, share, loop, 0)
            pl.when(jnp.logical_not(owner))(lambda: do(0))

        def by_owner(wait, call=lambda f: f()):
            call(lambda: pl.when(owner)(lambda: wait(share - 1)))
            call(lambda: pl.when(jnp.logical_not(owner))(lambda: wait(share)))

        def each_member(do):
            def loop(k, carry):
                do(k)
                return carry

            lax.fori_loop(1, members, loop, 0)

        for e in range(first, first + share):
            block = h_v[:, e * own_rows : (e + 1) * own_rows]
            hp[e] = jnp.concatenate([block, jnp.zeros((tokens, padded - own_rows), BF16)], axis=1)
            zs[0, e] = (fold(dot_nn(first3, hp[e]), 3) * scale).astype(BF16)

        for step in range(POWER):
            last = step == POWER - 1
            z_k = take(1)

            def z_send(k):
                to = fellow(k)
                send(zs.at[step, to], zr.at[step, me], z_k, dp=to)

            each_fellow(z_send)
            by_owner(
                lambda count, step=step, z_k=z_k: remote(
                    zs.at[step, pl.ds(0, count)], zs.at[step, pl.ds(0, count)], z_k, outer=1 - pod
                ).wait_send(),
                left_over.append,
            )

            def z_wait():
                pl.when(owner)(lambda: came(zr.at[step, pl.ds(0, members - 1)], z_k))

            yield z_wait

            left_k = take(2)

            @pl.when(owner)
            def _():
                zr[step, me] = zs[step, me]
                left = orthonormal(jnp.sum(zr[step].astype(F32), axis=0))
                if last:
                    atom = lax.broadcasted_iota(jnp.int32, (atoms, 1), 0)
                    left = jnp.where(atom < kept_ref[0, 0], left, 0.0)
                rounded = left.astype(BF16)
                ls[step] = rounded
                lr[step, me] = rounded

                def left_send(k):
                    send(ls.at[step], lr.at[step, me], left_k, left_k + 1, dp=member(k))

                each_member(left_send)

            def left_sent(step=step, left_k=left_k):
                all_sent = lr.at[step, pl.ds(0, members - 1)]
                pl.when(owner)(lambda: remote(all_sent, all_sent, left_k, outer=1 - pod).wait_send())

            left_over.append(left_sent)

            def left_wait():
                by_owner(lambda count: came(lr.at[step, pl.ds(first, count)], left_k + 1))

            yield left_wait

            for e in range(first, first + share):
                block = (dot_nt(lr[step, e], hp[e]) * scale).astype(BF16)
                u_y[step, y, e * atoms : (e + 1) * atoms] = block
                u_z[step, z, e * atoms : (e + 1) * atoms] = block
            group_rows = pl.ds(first * atoms, share * atoms)
            waits = both(
                ring_gather(lambda i: u_y.at[step, i, group_rows], ring_y),
                ring_gather(lambda i: u_z.at[step, i, group_rows], ring_z),
            )
            if last:
                own_left = pltpu.make_async_copy(
                    lr.at[step, pl.ds(first, share)],
                    left_out.at[pl.ds(first, share), pod],
                    local_sems.at[5 + g],
                )
                own_left.start()
                left_over.append(own_left.wait)
                k = take(1)
                send(
                    lr.at[step, pl.ds(first, share)],
                    left_out.at[pl.ds(first, share), pod],
                    k,
                    outer=1 - pod,
                )
                other_left = left_out.at[pl.ds(first, share), 1 - pod]
                went(other_left, k)
                left_over.append(lambda k=k, ref=other_left: came(ref, k))
            yield waits

            regroup_wait()
            for u, o, v in ((u_y, o_a, v_a), (u_z, o_b, v_b)):
                total = dot_nn(u[step, 0, rows], o[0])
                for c in range(1, SIDE):
                    total = total + dot_nn(u[step, c, rows], o[c])
                v[step, g] = total.astype(BF16).reshape(v.shape[2:])
            wait_a, total_a = ring_sum(v_a.at[step, g], rs_v.at[step, g, 0], ring_z)
            wait_b, total_b = ring_sum(v_b.at[step, g], rs_v.at[step, g, 1], ring_y)
            yield both(wait_a, wait_b)
            if last:
                break
            va_full[g, z] = total_a().astype(BF16)
            vb_full[g, y] = total_b().astype(BF16)
            yield both(
                ring_gather(lambda i: va_full.at[g, i], ring_z),
                ring_gather(lambda i: vb_full.at[g, i], ring_y),
            )
            for v, o, w in ((va_full, o_a, w_a), (vb_full, o_b, w_b)):
                whole = v[g].reshape(share * atoms, quarter)
                for c in range(SIDE):
                    w[g, c] = dot_nt(whole, o[c]).astype(BF16)
            wait_a, total_a = ring_sum(w_a.at[g], rs_w.at[g, 0], ring_y)
            wait_b, total_b = ring_sum(w_b.at[g], rs_w.at[g, 1], ring_z)
            yield both(wait_a, wait_b)
            token_side = total_a() + total_b()
            for i in range(share):
                pair = split2(token_side[i * atoms : (i + 1) * atoms])
                zs[step + 1, first + i] = (fold(dot_nn(pair, hp[first + i]), 2) * scale).astype(BF16)

        f1[g, 0] = total_a().astype(BF16).reshape(f1.shape[2:])
        f1[g, 1] = total_b().astype(BF16).reshape(f1.shape[2:])
        for i, shift in enumerate(SHIFTS):
            send(f1.at[g, 0], f2.at[y, z, g, :, pod], row_k, row_k + i, dp=ring_z.peer(shift), outer=0)
            send(f1.at[g, 1], f2.at[z, y, g, :, pod], row_k, row_k + i, dp=ring_y.peer(shift), outer=1)
        send(f1.at[g, 1 - pod], f2.at[row, col, g, :, pod], cross_k, outer=1 - pod)
        f2[col, row, g, :, pod] = f1[g, pod]

    row, col = rows_ring.place, cols_ring.place
    row_k, cross_k, unit_k, far_k = take(len(SHIFTS)), take(1), take(2 * SIDE), take(SIDE)

    chains = [piece_chain(g) for g in range(GROUPS)]
    waits = [lambda: None] * GROUPS
    cycle = 0
    while any(wait is not None for wait in waits):
        for g in range(GROUPS):
            if waits[g] is not None:
                waits[g]()
                waits[g] = next(chains[g], None)
        cycle += 1
        if cycle < len(ROUNDS):
            regroup_rounds(ROUNDS[cycle])
        if cycle == CUT:
            for wait in waits:
                if wait is not None:
                    wait()
            regroup_wait()
            break
    if CUT is None:
        went(f2.at[0, pl.ds(0, 3)], row_k)

        def go(shift, slot, which, to, recv):
            ref = f2.at[cols_ring.at(shift), slot, :, :, which]
            send(ref, ref, far_k, recv, dp=cols_ring.peer(to))

        def unit_start(slot, i):
            go(0, slot, 0, 1, unit_k + 2 * i)
            go(0, slot, 1, -1, unit_k + 2 * i + 1)
            go(0, slot, 1, 1, far_k + i)
            go(0, slot, 0, -1, far_k + i)

        def unit_forward(slot, i):
            came(f2.at[cols_ring.at(-1), slot, :, :, 0], unit_k + 2 * i)
            go(-1, slot, 0, 1, far_k + i)
            came(f2.at[cols_ring.at(1), slot, :, :, 1], unit_k + 2 * i + 1)
            go(1, slot, 1, -1, far_k + i)

        def unit_done(slot, i):
            came(f2.at[pl.ds(0, 2), slot], far_k + i)
            out = pltpu.make_async_copy(
                f2.at[:, slot], right_out.at[:, slot], local_sems.at[5 + GROUPS + i]
            )
            out.start()
            left_over.append(out.wait)

        came(f2.at[col, row, :, :, 1 - pod], cross_k)
        went(f2.at[col, row, :, :, 1 - pod], cross_k)
        unit_start(row, 0)
        slots = [row]
        for i, shift in enumerate(SHIFTS):
            slots.append(rows_ring.at(-shift))
            came(f2.at[col, slots[-1]], row_k + i)
            unit_start(slots[-1], i + 1)
            unit_forward(slots[-2], i)
            if i > 0:
                unit_done(slots[i - 1], i - 1)
        unit_forward(slots[-1], SIDE - 1)
        unit_done(slots[-2], SIDE - 2)
        unit_done(slots[-1], SIDE - 1)
        went(f2.at[pl.ds(0, 3)], far_k)
    for wait in left_over:
        wait()


def rebuild_kernel(left_hbm, right_hbm, out_hbm, left_v, right_v, out_v, sems):
    pieces, own_rows, _ = out_v.shape
    per_row = pieces // GROUPS // SIDE

    def place(e):
        group, rest = divmod(e, pieces // GROUPS)
        return rest // per_row * (pieces // SIDE) + group * per_row + rest % per_row

    width = right_v.shape[-1]
    load_left = pltpu.make_async_copy(left_hbm, left_v, sems.at[2 * pieces])
    load_left.start()
    loads = [pltpu.make_async_copy(right_hbm.at[:, place(e)], right_v.at[:, e], sems.at[e]) for e in range(pieces)]
    stores = [
        pltpu.make_async_copy(out_v.at[e], out_hbm.at[pl.ds(e * own_rows, own_rows)], sems.at[pieces + e])
        for e in range(pieces)
    ]
    for load in loads:
        load.start()
    load_left.wait()
    for e in range(pieces):
        left = left_v[e].reshape(-1, left_v.shape[-1])[:, :own_rows]
        loads[e].wait()
        for c in range(SIDE):
            right = right_v[c, e].reshape(left.shape[0], width)
            out_v[e, :, c * width : (c + 1) * width] = lax.dot_general(
                left, right, TN, preferred_element_type=F32
            ).astype(BF16)
        stores[e].start()
    for store in stores:
        store.wait()


def shards(hidden_act, out_grad, start_vectors, kept_counts):
    tokens, features = out_grad.shape
    atoms = start_vectors.shape[0]
    members = lax.axis_size("dp")
    pods = lax.axis_size("outer")
    hidden_rows = hidden_act.shape[1]
    own_rows = hidden_rows // members
    padded = -(-own_rows // LANES) * LANES
    quarter = features // 2 // SIDE
    share = members // GROUPS
    part = share * atoms // SIDE
    per_row = share // SIDE
    scale = 1.0 / math.sqrt(tokens * members)
    any_space = pl.BlockSpec(memory_space=pl.ANY)
    sem_count = 6 + GROUPS * (POWER * 7 + 5) + 16
    right_atoms, left_atoms = pl.pallas_call(
        functools.partial(chain, members, atoms, own_rows, scale),
        out_shape=(
            jax.ShapeDtypeStruct((SIDE, SIDE, GROUPS, per_row, pods, atoms, quarter), BF16),
            jax.ShapeDtypeStruct((members, pods, atoms, padded), BF16),
        ),
        in_specs=[any_space, any_space, any_space, pl.BlockSpec(memory_space=pltpu.SMEM)],
        out_specs=(any_space, any_space),
        scratch_shapes=[
            pltpu.VMEM((tokens, hidden_rows), BF16),
            pltpu.VMEM((tokens, features), BF16),
            pltpu.VMEM((atoms, features), F32),
            pltpu.VMEM((members, tokens, padded), BF16),
            pltpu.VMEM((SIDE, tokens, quarter), BF16),
            pltpu.VMEM((SIDE, tokens, quarter), BF16),
            pltpu.VMEM((POWER, members, atoms, padded), BF16),
            pltpu.VMEM((POWER, members, atoms, padded), BF16),
            pltpu.VMEM((POWER, atoms, padded), BF16),
            pltpu.VMEM((POWER, members, atoms, padded), BF16),
            pltpu.VMEM((POWER, SIDE, members * atoms, tokens), BF16),
            pltpu.VMEM((POWER, SIDE, members * atoms, tokens), BF16),
            pltpu.VMEM((POWER, GROUPS, SIDE, part, quarter), BF16),
            pltpu.VMEM((POWER, GROUPS, SIDE, part, quarter), BF16),
            pltpu.VMEM((GROUPS, SIDE, part, quarter), BF16),
            pltpu.VMEM((GROUPS, SIDE, part, quarter), BF16),
            pltpu.VMEM((GROUPS, SIDE, share * atoms, tokens), BF16),
            pltpu.VMEM((GROUPS, SIDE, share * atoms, tokens), BF16),
            pltpu.VMEM((POWER, GROUPS, 2, 3, part, quarter), BF16),
            pltpu.VMEM((GROUPS, 2, 3, share * atoms, tokens), BF16),
            pltpu.VMEM((GROUPS, 2, per_row, atoms, quarter), BF16),
            pltpu.VMEM((SIDE, SIDE, GROUPS, per_row, pods, atoms, quarter), BF16),
            pltpu.SemaphoreType.DMA((sem_count,)),
            pltpu.SemaphoreType.DMA((sem_count,)),
            pltpu.SemaphoreType.DMA((5 + GROUPS + SIDE,)),
        ],
        compiler_params=pltpu.CompilerParams(
            collective_id=0, has_side_effects=True, vmem_limit_bytes=VMEM_BYTES
        ),
        name="power_chain",
    )(hidden_act, out_grad, start_vectors, kept_counts.reshape(1, 1))
    return pl.pallas_call(
        rebuild_kernel,
        out_shape=jax.ShapeDtypeStruct((hidden_rows, features // pods), BF16),
        in_specs=[any_space, any_space],
        out_specs=any_space,
        scratch_shapes=[
            pltpu.VMEM((members, pods, atoms, padded), BF16),
            pltpu.VMEM((SIDE, members, pods, atoms, quarter), BF16),
            pltpu.VMEM((members, own_rows, features // pods), BF16),
            pltpu.SemaphoreType.DMA((2 * members + 1,)),
        ],
        compiler_params=pltpu.CompilerParams(vmem_limit_bytes=VMEM_BYTES),
        name="rebuild",
    )(left_atoms, right_atoms.reshape(SIDE, members, pods, atoms, quarter))


def solution(mesh):
    placed = (
        P(("dp", "outer"), "tensor"),
        P(("dp", "outer"), None),
        P(),
        P("tensor", "outer", "dp"),
    )
    return jax.shard_map(
        shards, mesh=mesh, in_specs=placed, out_specs=P("tensor", "outer"), check_vma=False
    )
```

```python
import functools
import math

import jax
import jax.numpy as jnp
from jax import lax
from jax.experimental import pallas as pl
from jax.experimental.pallas import tpu as pltpu
from jax.sharding import PartitionSpec as P

POWER = 2
SIDE = 4
LANES = 128
GROUPS = 4
CHUNKS = 4
ROUNDS = (2, 1, 1)
CUT = None
VMEM_BYTES = 60 * 1024 * 1024

F32 = jnp.float32
BF16 = jnp.bfloat16
NT = (((1,), (1,)), ((), ()))
TN = (((0,), (0,)), ((), ()))


def dot_nt(a, b):
    return lax.dot_general(a, b, NT, preferred_element_type=F32)


def dot_nn(a, b):
    return jnp.dot(a, b, preferred_element_type=F32)


def split2(x):
    high = x.astype(BF16)
    return jnp.concatenate([high, (x - high.astype(F32)).astype(BF16)], axis=0)


def split3(x):
    high = x.astype(BF16)
    rest = x - high.astype(F32)
    middle = rest.astype(BF16)
    low = (rest - middle.astype(F32)).astype(BF16)
    return jnp.concatenate([high, middle, low], axis=0)


def fold(x, times):
    rows = x.shape[0] // times
    total = x[:rows]
    for i in range(1, times):
        total = total + x[i * rows : (i + 1) * rows]
    return total


def orthonormal(left):
    atoms = left.shape[0]
    gram = lax.dot_general(left, left, NT, precision=lax.Precision.HIGHEST, preferred_element_type=F32)
    row = lax.broadcasted_iota(jnp.int32, (atoms, atoms), 0)
    col = lax.broadcasted_iota(jnp.int32, (atoms, atoms), 1)
    diagonal = row == col
    ridge = 1e-05 * jnp.sum(jnp.where(diagonal, gram, 0.0)) / atoms
    gram = gram + jnp.where(diagonal, ridge, 0.0)
    below = lax.broadcasted_iota(jnp.int32, (atoms, 1), 0)
    for j in range(atoms - 1):
        factor = jnp.where(below > j, gram[:, j : j + 1] / gram[j : j + 1, j : j + 1], 0.0)
        left = left - factor * left[j : j + 1]
        gram = gram - factor * gram[j : j + 1]
    pivots = jnp.sum(jnp.where(diagonal, gram, 0.0), axis=1, keepdims=True)
    return left / jnp.sqrt(pivots)


class Ring:
    def __init__(self, place, member):
        self.place, self.member = place, member

    def at(self, shift):
        return lax.rem(self.place + shift + SIDE, SIDE)

    def peer(self, shift):
        return self.member(self.at(shift))


SHIFTS = (2, 1, 3)


def chain(
    members,
    atoms,
    own_rows,
    scale,
    h_hbm,
    o_hbm,
    s_hbm,
    kept_ref,
    right_out,
    left_out,
    h_v,
    o_v,
    s_v,
    hp,
    o_a,
    o_b,
    zs,
    zr,
    ls,
    lr,
    u_y,
    u_z,
    v_a,
    v_b,
    va_full,
    vb_full,
    w_a,
    w_b,
    rs_v,
    rs_w,
    f1,
    f2,
    send_sems,
    recv_sems,
    local_sems,
):
    me = lax.axis_index("dp")
    pod = lax.axis_index("outer")
    y, z = lax.rem(me, SIDE), me // SIDE
    ring_y = Ring(y, lambda i: z * SIDE + i)
    ring_z = Ring(z, lambda i: i * SIDE + y)
    rows_ring = Ring(z + pod * (y - z), lambda i: (1 - pod) * (i * SIDE + y) + pod * (z * SIDE + i))
    cols_ring = Ring(y + pod * (z - y), lambda i: (1 - pod) * (z * SIDE + i) + pod * (i * SIDE + y))
    tokens, features = o_v.shape
    half = features // 2
    quarter = half // SIDE
    padded = hp.shape[2]
    share = members // GROUPS
    left_over = []
    taken = [0]

    def take(count):
        taken[0] += count
        return taken[0] - count

    def remote(src, dst, k, recv=None, **device):
        return pltpu.make_async_remote_copy(
            src_ref=src,
            dst_ref=dst,
            send_sem=send_sems.at[k],
            recv_sem=recv_sems.at[k if recv is None else recv],
            device_id=device,
            device_id_type=pl.DeviceIdType.MESH,
        )

    def send(src, dst, k, recv=None, **device):
        remote(src, dst, k, recv, **device).start()

    def came(dst, k):
        remote(dst, dst, k, outer=1 - pod).wait_recv()

    def went(src, k):
        left_over.append(lambda: remote(src, src, k, outer=1 - pod).wait_send())

    def member(shift):
        return lax.rem(me + shift + members, members)

    load_o = pltpu.make_async_copy(o_hbm, o_v, local_sems.at[0])
    load_h = pltpu.make_async_copy(h_hbm, h_v, local_sems.at[1])
    load_s = pltpu.make_async_copy(s_hbm, s_v, local_sems.at[2])
    load_s.start()
    load_o.start()
    load_h.start()

    barrier = pltpu.get_barrier_semaphore()

    def greet(**device):
        pl.semaphore_signal(barrier, inc=1, device_id=device, device_id_type=pl.DeviceIdType.MESH)

    def greet_member(k, carry):
        greet(dp=member(k))
        return carry

    lax.fori_loop(1, members, greet_member, 0)
    greet(outer=1 - pod)
    for shift in SHIFTS:
        greet(dp=ring_y.peer(shift), outer=1 - pod)
        greet(dp=ring_z.peer(shift), outer=1 - pod)
    load_s.wait()
    start3 = split3(s_v[...])
    load_o.wait()
    pl.semaphore_wait(barrier, members + 2 * len(SHIFTS))

    regroup_base = take(2 * len(SHIFTS))
    plan = [
        (regroup_base + 2 * i + j, shift, ring, first, buf)
        for i, shift in enumerate(SHIFTS)
        for j, (ring, first, buf) in enumerate(((ring_y, 0, o_a), (ring_z, half, o_b)))
    ]
    rounds = [0]

    def regroup_rounds(count):
        rows = tokens // CHUNKS
        for r in range(rounds[0], min(rounds[0] + count, CHUNKS)):
            for k, shift, ring, first, buf in plan:
                begin = pl.multiple_of(first + ring.at(shift) * quarter, quarter)
                remote(
                    o_v.at[pl.ds(r * rows, rows), pl.ds(begin, quarter)],
                    buf.at[ring.place, pl.ds(r * rows, rows)],
                    k,
                    dp=ring.peer(shift),
                ).start()
        rounds[0] = min(rounds[0] + count, CHUNKS)

    def regroup_wait():
        if rounds[0] is None:
            return
        regroup_rounds(CHUNKS)
        rounds[0] = None
        for k, shift, ring, first, buf in plan:
            came(buf.at[ring.at(-shift)], k)
            went(buf.at[ring.place], k)
        own_a.wait()
        own_b.wait()

    regroup_rounds(ROUNDS[0])
    own_a = pltpu.make_async_copy(
        o_v.at[:, pl.ds(pl.multiple_of(y * quarter, quarter), quarter)], o_a.at[y], local_sems.at[3]
    )
    own_b = pltpu.make_async_copy(
        o_v.at[:, pl.ds(pl.multiple_of(half + z * quarter, quarter), quarter)], o_b.at[z], local_sems.at[4]
    )
    own_a.start()
    own_b.start()

    first3 = split3(fold(dot_nt(start3, o_v[...]), 3))
    load_h.wait()

    def ring_gather(buf, ring):
        k = take(1)
        own = buf(ring.place)
        for shift in SHIFTS:
            send(own, own, k, dp=ring.peer(shift))
        three = buf(pl.ds(0, len(SHIFTS)))
        went(three, k)
        return lambda: came(three, k)

    def ring_sum(parts, land, ring):
        k = take(1)
        for i, shift in enumerate(SHIFTS):
            send(parts.at[ring.at(shift)], land.at[i], k, dp=ring.peer(shift))
        went(land, k)

        def wait():
            came(land, k)

        def total():
            value = parts[ring.place].astype(F32)
            for i in range(len(SHIFTS)):
                value = value + land[i].astype(F32)
            return value

        return wait, total

    def both(*waits):
        def wait():
            for one in waits:
                one()

        return wait

    def piece_chain(g):
        owner = me // share == g
        first = g * share
        rows = slice(first * atoms, (first + share) * atoms)

        def fellow(k):
            return first + lax.rem(lax.rem(me, share) + k, share)

        def each_fellow(do):
            def loop(k, carry):
                do(k)
                return carry

            lax.fori_loop(1, share, loop, 0)
            pl.when(jnp.logical_not(owner))(lambda: do(0))

        def by_owner(wait, call=lambda f: f()):
            call(lambda: pl.when(owner)(lambda: wait(share - 1)))
            call(lambda: pl.when(jnp.logical_not(owner))(lambda: wait(share)))

        def each_member(do):
            def loop(k, carry):
                do(k)
                return carry

            lax.fori_loop(1, members, loop, 0)

        for e in range(first, first + share):
            block = h_v[:, e * own_rows : (e + 1) * own_rows]
            hp[e] = jnp.concatenate([block, jnp.zeros((tokens, padded - own_rows), BF16)], axis=1)
            zs[0, e] = (fold(dot_nn(first3, hp[e]), 3) * scale).astype(BF16)

        for step in range(POWER):
            last = step == POWER - 1
            z_k = take(1)

            def z_send(k):
                to = fellow(k)
                send(zs.at[step, to], zr.at[step, me], z_k, dp=to)

            each_fellow(z_send)
            by_owner(
                lambda count, step=step, z_k=z_k: remote(
                    zs.at[step, pl.ds(0, count)], zs.at[step, pl.ds(0, count)], z_k, outer=1 - pod
                ).wait_send(),
                left_over.append,
            )

            def z_wait():
                pl.when(owner)(lambda: came(zr.at[step, pl.ds(0, members - 1)], z_k))

            yield z_wait

            left_k = take(2)

            @pl.when(owner)
            def _():
                zr[step, me] = zs[step, me]
                left = orthonormal(jnp.sum(zr[step].astype(F32), axis=0))
                if last:
                    atom = lax.broadcasted_iota(jnp.int32, (atoms, 1), 0)
                    left = jnp.where(atom < kept_ref[0, 0], left, 0.0)
                rounded = left.astype(BF16)
                ls[step] = rounded
                lr[step, me] = rounded

                def left_send(k):
                    send(ls.at[step], lr.at[step, me], left_k, left_k + 1, dp=member(k))

                each_member(left_send)

            def left_sent(step=step, left_k=left_k):
                all_sent = lr.at[step, pl.ds(0, members - 1)]
                pl.when(owner)(lambda: remote(all_sent, all_sent, left_k, outer=1 - pod).wait_send())

            left_over.append(left_sent)

            def left_wait():
                by_owner(lambda count: came(lr.at[step, pl.ds(first, count)], left_k + 1))

            yield left_wait

            for e in range(first, first + share):
                block = (dot_nt(lr[step, e], hp[e]) * scale).astype(BF16)
                u_y[step, y, e * atoms : (e + 1) * atoms] = block
                u_z[step, z, e * atoms : (e + 1) * atoms] = block
            group_rows = pl.ds(first * atoms, share * atoms)
            waits = both(
                ring_gather(lambda i: u_y.at[step, i, group_rows], ring_y),
                ring_gather(lambda i: u_z.at[step, i, group_rows], ring_z),
            )
            if last:
                own_left = pltpu.make_async_copy(
                    lr.at[step, pl.ds(first, share)],
                    left_out.at[pl.ds(first, share), pod],
                    local_sems.at[5 + g],
                )
                own_left.start()
                left_over.append(own_left.wait)
                k = take(1)
                send(
                    lr.at[step, pl.ds(first, share)],
                    left_out.at[pl.ds(first, share), pod],
                    k,
                    outer=1 - pod,
                )
                other_left = left_out.at[pl.ds(first, share), 1 - pod]
                went(other_left, k)
                left_over.append(lambda k=k, ref=other_left: came(ref, k))
            yield waits

            regroup_wait()
            for u, o, v in ((u_y, o_a, v_a), (u_z, o_b, v_b)):
                total = dot_nn(u[step, 0, rows], o[0])
                for c in range(1, SIDE):
                    total = total + dot_nn(u[step, c, rows], o[c])
                v[step, g] = total.astype(BF16).reshape(v.shape[2:])
            wait_a, total_a = ring_sum(v_a.at[step, g], rs_v.at[step, g, 0], ring_z)
            wait_b, total_b = ring_sum(v_b.at[step, g], rs_v.at[step, g, 1], ring_y)
            yield both(wait_a, wait_b)
            if last:
                break
            va_full[g, z] = total_a().astype(BF16)
            vb_full[g, y] = total_b().astype(BF16)
            yield both(
                ring_gather(lambda i: va_full.at[g, i], ring_z),
                ring_gather(lambda i: vb_full.at[g, i], ring_y),
            )
            for v, o, w in ((va_full, o_a, w_a), (vb_full, o_b, w_b)):
                whole = v[g].reshape(share * atoms, quarter)
                for c in range(SIDE):
                    w[g, c] = dot_nt(whole, o[c]).astype(BF16)
            wait_a, total_a = ring_sum(w_a.at[g], rs_w.at[g, 0], ring_y)
            wait_b, total_b = ring_sum(w_b.at[g], rs_w.at[g, 1], ring_z)
            yield both(wait_a, wait_b)
            token_side = total_a() + total_b()
            for i in range(share):
                pair = split2(token_side[i * atoms : (i + 1) * atoms])
                zs[step + 1, first + i] = (fold(dot_nn(pair, hp[first + i]), 2) * scale).astype(BF16)

        f1[g, 0] = total_a().astype(BF16).reshape(f1.shape[2:])
        f1[g, 1] = total_b().astype(BF16).reshape(f1.shape[2:])
        for i, shift in enumerate(SHIFTS):
            send(f1.at[g, 0], f2.at[y, z, g, :, pod], row_k, row_k + i, dp=ring_z.peer(shift), outer=0)
            send(f1.at[g, 1], f2.at[z, y, g, :, pod], row_k, row_k + i, dp=ring_y.peer(shift), outer=1)
        send(f1.at[g, 1 - pod], f2.at[row, col, g, :, pod], cross_k, outer=1 - pod)
        f2[col, row, g, :, pod] = f1[g, pod]

    row, col = rows_ring.place, cols_ring.place
    row_k, cross_k, unit_k, far_k = take(len(SHIFTS)), take(1), take(2 * SIDE), take(SIDE)

    chains = [piece_chain(g) for g in range(GROUPS)]
    waits = [lambda: None] * GROUPS
    cycle = 0
    while any(wait is not None for wait in waits):
        for g in range(GROUPS):
            if waits[g] is not None:
                waits[g]()
                waits[g] = next(chains[g], None)
        cycle += 1
        if cycle < len(ROUNDS):
            regroup_rounds(ROUNDS[cycle])
        if cycle == CUT:
            for wait in waits:
                if wait is not None:
                    wait()
            regroup_wait()
            break
    if CUT is None:
        went(f2.at[0, pl.ds(0, 3)], row_k)

        def go(shift, slot, which, to, recv):
            ref = f2.at[cols_ring.at(shift), slot, :, :, which]
            send(ref, ref, far_k, recv, dp=cols_ring.peer(to))

        def unit_start(slot, i):
            go(0, slot, 0, 1, unit_k + 2 * i)
            go(0, slot, 1, -1, unit_k + 2 * i + 1)
            go(0, slot, 1, 1, far_k + i)
            go(0, slot, 0, -1, far_k + i)

        def unit_forward(slot, i):
            came(f2.at[cols_ring.at(-1), slot, :, :, 0], unit_k + 2 * i)
            go(-1, slot, 0, 1, far_k + i)
            came(f2.at[cols_ring.at(1), slot, :, :, 1], unit_k + 2 * i + 1)
            go(1, slot, 1, -1, far_k + i)

        def unit_done(slot, i):
            came(f2.at[pl.ds(0, 2), slot], far_k + i)
            out = pltpu.make_async_copy(
                f2.at[:, slot], right_out.at[:, slot], local_sems.at[5 + GROUPS + i]
            )
            out.start()
            left_over.append(out.wait)

        came(f2.at[col, row, :, :, 1 - pod], cross_k)
        went(f2.at[col, row, :, :, 1 - pod], cross_k)
        unit_start(row, 0)
        slots = [row]
        for i, shift in enumerate(SHIFTS):
            slots.append(rows_ring.at(-shift))
            came(f2.at[col, slots[-1]], row_k + i)
            unit_start(slots[-1], i + 1)
            unit_forward(slots[-2], i)
            if i > 0:
                unit_done(slots[i - 1], i - 1)
        unit_forward(slots[-1], SIDE - 1)
        unit_done(slots[-2], SIDE - 2)
        unit_done(slots[-1], SIDE - 1)
        went(f2.at[pl.ds(0, 3)], far_k)
    for wait in left_over:
        wait()


def rebuild_kernel(left_hbm, right_hbm, out_hbm, left_v, right_v, out_v, sems):
    pieces, own_rows, _ = out_v.shape
    per_row = pieces // GROUPS // SIDE

    def place(e):
        group, rest = divmod(e, pieces // GROUPS)
        return rest // per_row * (pieces // SIDE) + group * per_row + rest % per_row

    width = right_v.shape[-1]
    load_left = pltpu.make_async_copy(left_hbm, left_v, sems.at[2 * pieces])
    load_left.start()
    loads = [pltpu.make_async_copy(right_hbm.at[:, place(e)], right_v.at[:, e], sems.at[e]) for e in range(pieces)]
    stores = [
        pltpu.make_async_copy(out_v.at[e], out_hbm.at[pl.ds(e * own_rows, own_rows)], sems.at[pieces + e])
        for e in range(pieces)
    ]
    for load in loads:
        load.start()
    load_left.wait()
    for e in range(pieces):
        left = left_v[e].reshape(-1, left_v.shape[-1])[:, :own_rows]
        loads[e].wait()
        for c in range(SIDE):
            right = right_v[c, e].reshape(left.shape[0], width)
            out_v[e, :, c * width : (c + 1) * width] = lax.dot_general(
                left, right, TN, preferred_element_type=F32
            ).astype(BF16)
        stores[e].start()
    for store in stores:
        store.wait()


def shards(hidden_act, out_grad, start_vectors, kept_counts):
    tokens, features = out_grad.shape
    atoms = start_vectors.shape[0]
    members = lax.axis_size("dp")
    pods = lax.axis_size("outer")
    hidden_rows = hidden_act.shape[1]
    own_rows = hidden_rows // members
    padded = -(-own_rows // LANES) * LANES
    quarter = features // 2 // SIDE
    share = members // GROUPS
    part = share * atoms // SIDE
    per_row = share // SIDE
    scale = 1.0 / math.sqrt(tokens * members)
    any_space = pl.BlockSpec(memory_space=pl.ANY)
    sem_count = 6 + GROUPS * (POWER * 7 + 5) + 16
    right_atoms, left_atoms = pl.pallas_call(
        functools.partial(chain, members, atoms, own_rows, scale),
        out_shape=(
            jax.ShapeDtypeStruct((SIDE, SIDE, GROUPS, per_row, pods, atoms, quarter), BF16),
            jax.ShapeDtypeStruct((members, pods, atoms, padded), BF16),
        ),
        in_specs=[any_space, any_space, any_space, pl.BlockSpec(memory_space=pltpu.SMEM)],
        out_specs=(any_space, any_space),
        scratch_shapes=[
            pltpu.VMEM((tokens, hidden_rows), BF16),
            pltpu.VMEM((tokens, features), BF16),
            pltpu.VMEM((atoms, features), F32),
            pltpu.VMEM((members, tokens, padded), BF16),
            pltpu.VMEM((SIDE, tokens, quarter), BF16),
            pltpu.VMEM((SIDE, tokens, quarter), BF16),
            pltpu.VMEM((POWER, members, atoms, padded), BF16),
            pltpu.VMEM((POWER, members, atoms, padded), BF16),
            pltpu.VMEM((POWER, atoms, padded), BF16),
            pltpu.VMEM((POWER, members, atoms, padded), BF16),
            pltpu.VMEM((POWER, SIDE, members * atoms, tokens), BF16),
            pltpu.VMEM((POWER, SIDE, members * atoms, tokens), BF16),
            pltpu.VMEM((POWER, GROUPS, SIDE, part, quarter), BF16),
            pltpu.VMEM((POWER, GROUPS, SIDE, part, quarter), BF16),
            pltpu.VMEM((GROUPS, SIDE, part, quarter), BF16),
            pltpu.VMEM((GROUPS, SIDE, part, quarter), BF16),
            pltpu.VMEM((GROUPS, SIDE, share * atoms, tokens), BF16),
            pltpu.VMEM((GROUPS, SIDE, share * atoms, tokens), BF16),
            pltpu.VMEM((POWER, GROUPS, 2, 3, part, quarter), BF16),
            pltpu.VMEM((GROUPS, 2, 3, share * atoms, tokens), BF16),
            pltpu.VMEM((GROUPS, 2, per_row, atoms, quarter), BF16),
            pltpu.VMEM((SIDE, SIDE, GROUPS, per_row, pods, atoms, quarter), BF16),
            pltpu.SemaphoreType.DMA((sem_count,)),
            pltpu.SemaphoreType.DMA((sem_count,)),
            pltpu.SemaphoreType.DMA((5 + GROUPS + SIDE,)),
        ],
        compiler_params=pltpu.CompilerParams(
            collective_id=0, has_side_effects=True, vmem_limit_bytes=VMEM_BYTES
        ),
        name="power_chain",
    )(hidden_act, out_grad, start_vectors, kept_counts.reshape(1, 1))
    return pl.pallas_call(
        rebuild_kernel,
        out_shape=jax.ShapeDtypeStruct((hidden_rows, features // pods), BF16),
        in_specs=[any_space, any_space],
        out_specs=any_space,
        scratch_shapes=[
            pltpu.VMEM((members, pods, atoms, padded), BF16),
            pltpu.VMEM((SIDE, members, pods, atoms, quarter), BF16),
            pltpu.VMEM((members, own_rows, features // pods), BF16),
            pltpu.SemaphoreType.DMA((2 * members + 1,)),
        ],
        compiler_params=pltpu.CompilerParams(vmem_limit_bytes=VMEM_BYTES),
        name="rebuild",
    )(left_atoms, right_atoms.reshape(SIDE, members, pods, atoms, quarter))


def solution(mesh):
    placed = (
        P(("dp", "outer"), "tensor"),
        P(("dp", "outer"), None),
        P(),
        P("tensor", "outer", "dp"),
    )
    return jax.shard_map(
        shards, mesh=mesh, in_specs=placed, out_specs=P("tensor", "outer"), check_vma=False
    )
```
